32 devices in a mesh: group: 2 (over core), expert: 4 (over z), mp: 4 (over y, x).
Axes of the slice: x: 2, y: 2, z: 4, core: 2. Of those that a mesh axis runs over, the one named last changes fastest.
Arguments:
- rows: bfloat16 [2, 256, 2048], P('group', 'expert'), may hold values from -6 to 6
- route: int32 [2, 256, 2], P('group', 'expert'), may hold values from 0 to 3, all different within a row; in each aligned block of 64 rows (0 to 63, 64 to 127, ..., all dimensions but the last counted through in order) at most 64 rows name the same one
- gate_int: int32 [2, 256, 2], P('group', 'expert'), may hold values from 1 to 31
- moe_gain: float32 [2, 2048], P('group'), may hold values from 0.1 to 1.9
- w_in: bfloat16 [2, 4, 2048, 4096], P('group', 'expert', None, 'mp'), may hold values from -0.125 to 0.125
- w_out: bfloat16 [2, 4, 4096, 2048], P('group', 'expert', 'mp'), may hold values from -0.09375 to 0.09375
- attn_gain: float32 [2, 2048], P('group'), may hold values from 0.1 to 1.9
- attn_weight: bfloat16 [2, 2048, 2, 1024], P('group', None, None, 'mp'), may hold values from -0.125 to 0.125
- src_len: int32 [4, 6], P('expert'), may hold values from 1 to 16, 64 in all within a row
- target: int32 [4, 6], P('expert'), may hold values from 0 to 255, as said below
- cache: bfloat16 [256, 16, 2, 1024], P('expert', None, None, 'mp'), may hold values from -128 to 128
- cache_len: int32 [256], P('expert'), may hold values from 1 to 16
Outputs:
- moe_out: bfloat16 [2, 256, 2048], P('group', 'expert')
- step_out: bfloat16 [2, 256, 2048], P('group', 'expert')
The draws below stay inside these ranges and needn't reach their ends.
Inputs may be any that keep to these rules, and one draw needn't show every extreme that they name: `route`: the rows of one device name one expert at most 64 times. `src_len`: the 6 lengths of one row sum to 64. `target`: all targets are different slots.
All inputs are finite; a program needn't handle non-finite values.
Results may differ from the reference program's by a relative error of at most 0.035.
Values may be sent and summed in bfloat16 or wider, within the bound.
A program may use at most 64 MiB of HBM per device.

```python
import math
import jax
import jax.numpy as jnp
import numpy as np
from jax import lax

D = 2048
HEADS = 8
HEAD_DIM = 128
FFW = 4096
ROWS = 64
SRC_DEV = 6
SRC_MAX = 16
EXPERTS = 4
CAPACITY = 64
TOKENS = 256
N_EXPERT = 4


def draw_target(key, part):
    key = jax.random.fold_in(key, 11)
    offset_key, order_key = jax.random.split(key)
    count = N_EXPERT
    extra = jax.random.randint(offset_key, (SRC_DEV,), 0, count).astype(jnp.int32)
    fixed_offsets = jnp.array([0, 1, count - 1, count // 2], jnp.int32)
    column = jnp.arange(SRC_DEV, dtype=jnp.int32)
    padded = jnp.concatenate([fixed_offsets, jnp.zeros((SRC_DEV,), jnp.int32)])[:SRC_DEV]
    offsets = jnp.where(column < 4, padded, extra)
    order_keys = jax.random.split(order_key, count)
    orders = jax.vmap(lambda one: jax.random.permutation(one, ROWS))(order_keys).astype(jnp.int32)
    encoder_index = jnp.arange(count, dtype=jnp.int32)[:, None]
    destination = (encoder_index + offsets[None, :]) % count
    local = orders[destination, column[None, :]]
    return (destination * ROWS + local).astype(jnp.int32)


def draw_cache(key, part):
    key = jax.random.fold_in(key, 23)
    shape = (ROWS * N_EXPERT, SRC_MAX, 2, HEADS * HEAD_DIM)
    first_key = jax.random.fold_in(key, 0)
    values = jnp.clip(jax.random.normal(first_key, shape, jnp.float32), -6.0, 6.0)
    return values.astype(jnp.bfloat16)


def touch_ends(values, own_key, least, largest):
    longest = values.shape.index(max(values.shape))
    spots = []
    for shift in (0, 1):
        where = [jax.random.randint(jax.random.fold_in(own_key, axis), (), 0, length) for axis, length in enumerate(values.shape)]
        where[longest] = (where[longest] + shift) % values.shape[longest]
        spots.append(tuple(where))
    return values.at[spots[0]].set(least).at[spots[1]].set(largest)


def shard_levels(own_key, dims, cuts, smallest, top_value):
    def one(axis_at, parts):
        steps = jax.random.uniform(jax.random.fold_in(jax.random.fold_in(own_key, 6), axis_at), (parts,), jnp.float32, smallest / len(cuts), top_value / len(cuts))
        return jnp.repeat(jnp.exp(steps), dims[axis_at] // parts).reshape((-1,) + (1,) * (len(dims) - axis_at - 1))

    factor_of = one(*cuts[0])
    for cut in cuts[1:]:
        factor_of = factor_of * one(*cut)
    return factor_of


def length_profile(amount, total, limit, slope):
    weights = [(1 << 20) // math.isqrt(grade ** slope) + 1 for grade in range(2, amount + 1)]
    spare, holding = total - limit - (amount - 1), [1] * (amount - 1)
    while spare > 0:
        movable = [i for i in range(amount - 1) if holding[i] < limit]
        whole, budget = sum([weights[i] for i in movable]), spare
        for i in movable:
            more = min(limit - holding[i], max(1, budget * weights[i] // whole), spare)
            holding[i] = holding[i] + more
            spare = spare - more
    return np.array([limit] + holding)


def uneven(own_key, count, total, limit, skew):
    if count == 2:
        one = jax.random.randint(own_key, (), max(1, total - limit), min(limit, total - 1) + 1)
        return jnp.stack([one, total - one])
    tallies = jnp.asarray(length_profile(count, total, limit, skew), jnp.int32)
    couples = (count - 1) // 2
    source_of, sink = tallies[1:1 + 2 * couples:2], tallies[2:2 + 2 * couples:2]
    room = jnp.minimum(source_of - 1, limit - sink)
    passed = jax.random.randint(jax.random.fold_in(own_key, 1), (couples,), 0, 1 << 20) % (room + 1)
    tallies = tallies.at[1:1 + 2 * couples:2].set(source_of - passed).at[2:2 + 2 * couples:2].set(sink + passed)
    return tallies[jax.random.permutation(jax.random.fold_in(own_key, 2), count)]


def deal_out(stream_key, own, number, rows, amount, top, most, slope):
    order = jax.random.permutation(stream_key, amount)
    crowded, ordinary = load_shares(amount, rows * top, most, slope, True), load_shares(amount, rows * top, most, slope, False)
    places = jnp.arange(amount)

    def named(sizes, turn):
        used = int((sizes > 0).sum())
        fixed = max(1, used // 4)
        passed = fixed + (places - fixed + turn * (used - fixed)) % max(1, amount - fixed)
        return jnp.zeros((amount,), jnp.int32).at[order[jnp.where(places < fixed, places, passed)]].set(jnp.asarray(sizes, jnp.int32))

    sizes = jnp.where(number % 4 == 0, named(crowded, number // 4), named(ordinary, number - number // 4 - 1))
    mixed = jax.random.permutation(jax.random.fold_in(own, 3), amount)
    donor, sink = mixed[0:amount // 2 * 2:2], mixed[1:amount // 2 * 2:2]
    room = jnp.minimum(sizes[donor] - 1, most - sizes[sink]) // 2
    room = jnp.where((donor == order[0]) | (sink == order[0]) | (sizes[sink] == 0), 0, jnp.maximum(room, 0))
    passed = jax.random.randint(jax.random.fold_in(own, 4), (amount // 2,), 0, 1 << 20) % (room + 1)
    sizes = sizes.at[donor].add(-passed).at[sink].add(passed)
    members = jnp.searchsorted(jnp.cumsum(sizes), jnp.arange(rows * top), side="right").astype(jnp.int32)
    listing = members.reshape(top, rows).T
    listing = listing[jax.random.permutation(jax.random.fold_in(own, 1), rows)]
    turn = jax.random.randint(jax.random.fold_in(own, 2), (rows, 1), 0, top)
    return jnp.take_along_axis(listing, (jnp.arange(top)[None, :] + turn) % top, axis=1)


def load_shares(number_of, total, reach, lean, full):
    weights = [(1 << 20) // math.isqrt(grade ** lean) + 1 for grade in range(1, number_of + 1)]
    largest = reach if full else min(reach, max(-(-total // number_of), total * weights[0] // sum(weights)))
    least = 1 if total - largest >= number_of - 1 else 0
    counts, spare = [largest] + [least] * (number_of - 1), total - largest - least * (number_of - 1)
    while spare > 0:
        movable = [i for i in range(1, number_of) if counts[i] < largest] or [i for i in range(1, number_of) if counts[i] < reach]
        mass, remaining = sum([weights[i] for i in movable]), spare
        for i in movable:
            addition = min(reach - counts[i], max(1, remaining * weights[i] // mass), spare)
            counts[i] = counts[i] + addition
            spare = spare - addition
    return np.array(counts)


def bell_draw(rng, dims, scale, limit, shards=(), kind=jnp.bfloat16):
    entries = jax.random.normal(rng, dims, jnp.float32) * scale
    if len(shards) > 0:
        entries = shard_levels(rng, dims, shards, -0.22, 0.18) * entries
    return jnp.clip(entries, min=-limit, max=limit).astype(kind)


def setup_inputs(seed: int = 0) -> dict:
    key_of = jax.random.split(jax.random.key(seed), 13)
    rows = bell_draw(key_of[0], (2, TOKENS, D), 1.0, 6.0, ((0, 2), (1, 4)))
    route_keys = jax.random.split(jax.random.fold_in(key_of[1], 1), 2 * TOKENS // ROWS)
    route_turns = jax.random.permutation(jax.random.fold_in(key_of[1], 3), 2 * TOKENS // ROWS)
    route = jax.vmap(lambda own, number: deal_out(jax.random.fold_in(key_of[1], 2), own, number, ROWS, EXPERTS, 2, CAPACITY, 2))(route_keys, route_turns).reshape((2, TOKENS, 2))
    gate_int = touch_ends(jax.random.randint(key_of[2], (2, TOKENS, 2), 1, 32), jax.random.fold_in(key_of[2], 1), 1, 31).astype(jnp.int32)
    moe_gain = jnp.clip(1.0 + 0.18 * jax.random.normal(key_of[3], (2, D), jnp.float32), 0.1, 1.9)
    w_in = bell_draw(key_of[4], (2, EXPERTS, D, FFW), D ** -0.5, 0.125, ((0, 2), (1, 4), (3, 4)))
    w_out = bell_draw(key_of[5], (2, EXPERTS, FFW, D), FFW ** -0.5, 0.09375, ((0, 2), (1, 4), (2, 4)))
    attn_gain = jnp.clip(1.0 + 0.18 * jax.random.normal(key_of[6], (2, D), jnp.float32), 0.1, 1.9)
    attn_weight = bell_draw(key_of[7], (2, D, 2, HEADS * HEAD_DIM), D ** -0.5, 0.125, ((0, 2), (3, 4)))
    src_len = jax.vmap(lambda own: uneven(own, SRC_DEV, ROWS, SRC_MAX, 2))(jax.random.split(key_of[8], N_EXPERT)).reshape((N_EXPERT, SRC_DEV)).astype(jnp.int32)
    target = draw_target(jax.random.fold_in(key_of[12], 71), 0)
    cache = draw_cache(jax.random.fold_in(key_of[12], 71), 0)
    cache_len = touch_ends(jax.random.randint(key_of[11], (TOKENS,), 1, SRC_MAX + 1), jax.random.fold_in(key_of[11], 1), 1, SRC_MAX).astype(jnp.int32)
    return dict(rows=rows, route=route, gate_int=gate_int, moe_gain=moe_gain, w_in=w_in, w_out=w_out, attn_gain=attn_gain, attn_weight=attn_weight, src_len=src_len, target=target, cache=cache, cache_len=cache_len)


def layer_norm(values, gain):
    center = values - lax.optimization_barrier(jnp.mean(values, axis=-1, keepdims=True))
    spread = lax.optimization_barrier(jnp.mean(center * center, axis=-1, keepdims=True))
    return center * lax.rsqrt(spread + 1e-05) * gain

def expert_layer(block, routes, gates, gain, first, second):
    base = block.astype(jnp.float32)
    normed = layer_norm(base, gain).astype(jnp.bfloat16)
    weights = gates.astype(jnp.float32)
    weights = weights / lax.optimization_barrier(jnp.sum(weights, axis=1, keepdims=True))
    room = N_EXPERT * CAPACITY

    def one_expert(total, which):
        hit = routes == which
        picked = lax.optimization_barrier(jnp.sum(jnp.where(hit, weights, 0.0), axis=1))
        used = jnp.any(hit, axis=1)
        index = jnp.nonzero(used, size=room, fill_value=0)[0].astype(jnp.int32)
        valid = jnp.arange(room) < jnp.sum(used.astype(jnp.int32))
        hidden = jax.nn.relu(jnp.dot(normed[index], first[which], preferred_element_type=jnp.float32)).astype(jnp.bfloat16)
        result = jnp.dot(hidden, second[which], preferred_element_type=jnp.float32).astype(jnp.bfloat16).astype(jnp.float32)
        scale = jnp.where(valid, picked[index], 0.0)
        return (total.at[index].add(scale[:, None] * result), None)
    start = jnp.zeros(base.shape, jnp.float32)
    summed, _ = lax.scan(one_expert, start, jnp.arange(first.shape[0], dtype=jnp.int32))
    return (base + summed).astype(jnp.bfloat16)

def reference(rows, route, gate_int, moe_gain, w_in, w_out, attn_gain, attn_weight, src_len, target, cache, cache_len):
    encoder_rows = expert_layer(rows[0], route[0], gate_int[0], moe_gain[0], w_in[0], w_out[0])
    decoder_rows = expert_layer(rows[1], route[1], gate_int[1], moe_gain[1], w_in[1], w_out[1])
    width = HEADS * HEAD_DIM
    encoded = layer_norm(encoder_rows.astype(jnp.float32), attn_gain[0]).astype(jnp.bfloat16)
    new_kv = jnp.dot(encoded, attn_weight[0].reshape(D, 2 * width), preferred_element_type=jnp.float32)
    new_kv = new_kv.astype(jnp.bfloat16).reshape(TOKENS, 2, width)
    normed_dec = layer_norm(decoder_rows.astype(jnp.float32), attn_gain[1]).astype(jnp.bfloat16)
    query = jnp.dot(normed_dec, attn_weight[1][:, 0, :], preferred_element_type=jnp.float32).astype(jnp.bfloat16)
    ends = jnp.cumsum(src_len, axis=1)
    starts = ends - src_len + (jnp.arange(N_EXPERT, dtype=jnp.int32) * ROWS)[:, None]
    starts = starts.reshape(-1).astype(jnp.int32)
    lengths = src_len.reshape(-1).astype(jnp.int32)
    owner = jnp.full((TOKENS,), -1, jnp.int32).at[target.reshape(-1)].set(jnp.arange(N_EXPERT * SRC_DEV, dtype=jnp.int32))
    freed = owner >= 0
    own = jnp.maximum(owner, 0)
    source_rows = starts[own][:, None] + jnp.arange(SRC_MAX, dtype=jnp.int32)[None, :]
    source_rows = jnp.clip(source_rows, 0, TOKENS - 1).astype(jnp.int32)
    slot_kv = jnp.where(freed[:, None, None, None], new_kv[source_rows], cache)
    slot_len = jnp.where(freed, lengths[own], cache_len)
    keys = slot_kv[:, :, 0, :].reshape(TOKENS, SRC_MAX, HEADS, HEAD_DIM).astype(jnp.float32)
    values = slot_kv[:, :, 1, :].reshape(TOKENS, SRC_MAX, HEADS, HEAD_DIM).astype(jnp.float32)
    heads_query = query.reshape(TOKENS, HEADS, HEAD_DIM).astype(jnp.float32)
    scores = jnp.einsum('thd,tphd->thp', heads_query, keys) * (1.0 / math.sqrt(HEAD_DIM))
    inside = jnp.arange(SRC_MAX)[None, None, :] < slot_len[:, None, None]
    scores = jnp.where(inside, scores, -1e+30)
    highest = lax.optimization_barrier(jnp.max(scores, axis=-1, keepdims=True))
    raised = jnp.where(inside, jnp.exp(scores - highest), 0.0)
    probs = (raised / lax.optimization_barrier(jnp.sum(raised, axis=-1, keepdims=True))).astype(jnp.bfloat16)
    context = jnp.einsum('thp,tphd->thd', probs.astype(jnp.float32), values).astype(jnp.bfloat16).reshape(TOKENS, width)
    output_map = attn_weight[1][:, 1, :]
    mixed = jnp.dot(context, output_map.T, preferred_element_type=jnp.float32)
    decoded = (decoder_rows.astype(jnp.float32) + mixed).astype(jnp.bfloat16)
    return (jnp.stack([encoder_rows, decoder_rows]), jnp.stack([encoded, decoded]))
```

```python
import math

import jax
import jax.numpy as jnp
from jax import lax
from jax.experimental import pallas as pl
from jax.experimental.pallas import tpu as pltpu
from jax.sharding import PartitionSpec as P

HEAD_DIM = 128


def layer_norm(values, gain):
    center = values - jnp.mean(values, axis=-1, keepdims=True)
    spread = jnp.mean(center * center, axis=-1, keepdims=True)
    return center * lax.rsqrt(spread + 1e-05) * gain


def spread_body(
    rows,
    route,
    gate_int,
    moe_gain,
    w_in,
    w_out,
    attn_gain,
    attn_weight,
    src_len,
    target,
    cache,
    cache_len,
):
    experts_count = lax.axis_size("expert")
    row_count = rows.shape[1]
    width = rows.shape[2]
    group_place = lax.axis_index("group")
    expert_place = lax.axis_index("expert")
    capacity = max(2, 4 * row_count // experts_count)
    base = rows[0].astype(jnp.float32)
    normed = layer_norm(base, moe_gain[0]).astype(jnp.bfloat16)
    weights = gate_int[0].astype(jnp.float32)
    weights = weights / jnp.sum(weights, axis=1, keepdims=True)
    flat_dest = route[0].reshape(-1)
    onehot = (flat_dest[:, None] == jnp.arange(experts_count)[None, :]).astype(jnp.int32)
    position = jnp.sum((jnp.cumsum(onehot, axis=0) - 1) * onehot, axis=1)
    flat_index = flat_dest * capacity + position
    pair_index = flat_index.reshape(row_count, 2)
    slot_iota = jnp.arange(experts_count * capacity, dtype=jnp.int32)
    slot_table = (
        (slot_iota[:, None] == pair_index[None, :, 0])
        | (slot_iota[:, None] == pair_index[None, :, 1])
    ).astype(jnp.bfloat16)
    buffer = jnp.dot(slot_table, normed, preferred_element_type=jnp.float32).astype(jnp.bfloat16)
    buffer = buffer.reshape(experts_count, capacity, normed.shape[1])
    hidden = jax.nn.relu(
        jnp.einsum(
            "sci,if->scf",
            lax.all_to_all(buffer, "expert", split_axis=0, concat_axis=0, tiled=True),
            w_in[0, 0],
            preferred_element_type=jnp.float32,
        )
    ).astype(jnp.bfloat16)
    partial_rows = jnp.einsum(
        "scf,fo->sco", hidden, w_out[0, 0], preferred_element_type=jnp.float32
    )
    summed = lax.psum(partial_rows.astype(jnp.bfloat16), "mp")
    returned = lax.all_to_all(summed, "expert", split_axis=0, concat_axis=0, tiled=True)
    returned = returned.reshape(experts_count * capacity, returned.shape[2])
    picked = returned[flat_index].reshape(row_count, 2, returned.shape[1]).astype(jnp.float32)
    added = weights[:, 0:1] * picked[:, 0] + weights[:, 1:2] * picked[:, 1]
    moe_rows = (base + added).astype(jnp.bfloat16)
    encoded = layer_norm(moe_rows.astype(jnp.float32), attn_gain[0]).astype(jnp.bfloat16)
    head_width = attn_weight.shape[3]
    projected = jnp.dot(
        encoded, attn_weight[0].reshape(width, 2 * head_width), preferred_element_type=jnp.float32
    )
    projected = projected.reshape(row_count, 2, head_width).astype(jnp.bfloat16)
    query = projected[:, 0, :]
    lengths = src_len[0]
    ends = jnp.cumsum(lengths)
    starts = ends - lengths
    row_iota = jnp.arange(row_count, dtype=jnp.int32)
    which = jnp.sum((row_iota[:, None] >= ends[None, :]).astype(jnp.int32), axis=1)
    select = which[:, None] == jnp.arange(lengths.shape[0])[None, :]
    row_start = jnp.sum(jnp.where(select, starts[None, :], 0), axis=1)
    row_len = jnp.sum(jnp.where(select, lengths[None, :], 0), axis=1)
    row_slot = jnp.sum(jnp.where(select, target[0][None, :], 0), axis=1)
    row_pos = row_iota - row_start
    positions = cache.shape[1]
    cell_iota = jnp.arange(row_count * positions, dtype=jnp.int32)
    slot_ids = jnp.arange(row_count, dtype=jnp.int32)
    sent_slot = jnp.where(group_place == 0, row_slot, -1)
    slot_kv = cache
    slot_len = cache_len
    kv_piece = lax.all_gather(projected, ("group", "expert"), axis=0, tiled=True)
    slot_piece = lax.all_gather(sent_slot, ("group", "expert"), axis=0, tiled=True)
    pos_piece = lax.all_gather(row_pos, ("group", "expert"), axis=0, tiled=True)
    len_piece = lax.all_gather(row_len, ("group", "expert"), axis=0, tiled=True)
    local = slot_piece - expert_place * row_count
    inside = (local >= 0) & (local < row_count)
    cell = jnp.where(inside, local * positions + pos_piece, -1)
    hit = cell_iota[:, None] == cell[None, :]
    written = jnp.dot(
        hit.astype(jnp.bfloat16),
        kv_piece.reshape(kv_piece.shape[0], -1),
        preferred_element_type=jnp.float32,
    )
    written = written.astype(jnp.bfloat16).reshape(slot_kv.shape)
    touched = jnp.any(hit, axis=1).reshape(row_count, positions)
    slot_kv = jnp.where(touched[:, :, None, None], written, slot_kv)
    slot_hit = (slot_ids[:, None] == local[None, :]) & inside[None, :]
    fresh = jnp.max(jnp.where(slot_hit, len_piece[None, :], 0), axis=1).astype(jnp.int32)
    slot_len = jnp.where(jnp.any(slot_hit, axis=1), fresh, slot_len)
    slot_kv, slot_len = (slot_kv, slot_len)
    heads_here = head_width // HEAD_DIM
    keys = slot_kv[:, :, 0, :].reshape(row_count, positions, heads_here, HEAD_DIM)
    values = slot_kv[:, :, 1, :].reshape(row_count, positions, heads_here, HEAD_DIM)
    heads_query = query.reshape(row_count, heads_here, HEAD_DIM)
    scores = jnp.einsum("thd,tphd->thp", heads_query, keys, preferred_element_type=jnp.float32) * (
        1.0 / math.sqrt(HEAD_DIM)
    )
    inside = jnp.arange(positions)[None, None, :] < slot_len[:, None, None]
    scores = jnp.where(inside, scores, -1e30)
    highest = jnp.max(scores, axis=-1, keepdims=True)
    raised = jnp.where(inside, jnp.exp(scores - highest), 0.0)
    probs = (raised / jnp.sum(raised, axis=-1, keepdims=True)).astype(jnp.bfloat16)
    context = jnp.einsum("thp,tphd->thd", probs, values, preferred_element_type=jnp.float32).astype(
        jnp.bfloat16
    )
    context = context.reshape(row_count, head_width)
    output_map = attn_weight[0][:, 1, :]
    mixed = lax.dot_general(
        context, output_map, (((1,), (1,)), ((), ())), preferred_element_type=jnp.float32
    )
    mixed = lax.psum(mixed.astype(jnp.bfloat16), "mp").astype(jnp.float32)
    decoded = (moe_rows.astype(jnp.float32) + mixed).astype(jnp.bfloat16)
    step_rows = jnp.where(group_place == 0, encoded, decoded)
    return (moe_rows[None], step_rows[None])


MESH = pl.DeviceIdType.MESH
NT = (((1,), (1,)), ((), ()))


def norm_rows(values, gain):
    center = values - jnp.mean(values, axis=-1, keepdims=True)
    spread = jnp.mean(center * center, axis=-1, keepdims=True)
    return (center * lax.rsqrt(spread + 1e-05) * gain).astype(jnp.bfloat16)


def kernel(
    rows_ref, route_ref, gate_ref, moe_gain_ref, attn_gain_ref, src_ref, target_ref, cache_len_ref,
    w_in_hbm, w_out_hbm, attn_hbm, cache_hbm,
    moe_ref, step_ref,
    w_in, w_out, attn, cache, gathered, hidden, part, part_got, summed, back_got, moe, meta,
    kv, kv_got, slot_kv, mixed, mixed_got, final,
    load_sem, z_send, z_recv, m_send, m_recv, f_send, f_recv, p_send, p_recv, b_send, b_recv,
    e_send, e_recv, k_send, k_recv, g_send, g_recv, h_send, h_recv,
):
    g = lax.axis_index("group")
    e = lax.axis_index("expert")
    m = lax.axis_index("mp")
    n_expert = lax.axis_size("expert")
    row_count = rows_ref.shape[1]
    width = rows_ref.shape[2]
    quarter = width // 4
    head_width = attn.shape[1] // 2
    total = n_expert * row_count
    y, x = m // 2, m % 2
    mp_peer = (m, y * 2 + 1 - x, (1 - y) * 2 + x, 3 - m)
    ahead = [(e + d) % n_expert for d in range(n_expert)]
    behind = [(e + n_expert - d) % n_expert for d in range(n_expert)]

    loads = [
        pltpu.make_async_copy(w_in_hbm.at[0, 0], w_in, load_sem.at[0]),
        pltpu.make_async_copy(w_out_hbm.at[0, 0], w_out, load_sem.at[1]),
        pltpu.make_async_copy(attn_hbm, attn, load_sem.at[2]),
        pltpu.make_async_copy(cache_hbm, cache, load_sem.at[3]),
    ]
    barrier = pltpu.get_barrier_semaphore()
    friends = [(g, ahead[d], m) for d in range(1, n_expert)]
    friends += [(g, e, mp_peer[j]) for j in (1, 2, 3)]
    friends += [(1 - g, ahead[d], m) for d in range(n_expert)]
    for friend in friends:
        pl.semaphore_signal(barrier, inc=1, device_id=friend, device_id_type=MESH)
    for load in loads:
        load.start()

    def cols(place):
        return pl.ds(pl.multiple_of(place * quarter, quarter), quarter)

    def block(d):
        return pl.ds(d * row_count, row_count)

    def send(src, dst, send_sem, recv_sem, device):
        copy = pltpu.make_async_remote_copy(
            src_ref=src, dst_ref=dst, send_sem=send_sem, recv_sem=recv_sem,
            device_id=device, device_id_type=MESH,
        )
        return copy

    pending = []

    def go(*args):
        copy = send(*args)
        copy.start()
        pending.append(copy)

    base = rows_ref[0].astype(jnp.float32)
    gathered[block(0), :] = norm_rows(base, moe_gain_ref[...])
    meta[0] = jnp.zeros(meta.shape[1:], jnp.int32)
    meta[0, 0:1, 0:src_ref.shape[1]] = src_ref[...]
    meta[0, 1:2, 0:src_ref.shape[1]] = target_ref[...]
    pl.semaphore_wait(barrier, len(friends))

    for d in (2, 1, 3):
        go(gathered.at[block(0), cols(m)], gathered.at[block(d), cols(m)],
           z_send.at[d], z_recv.at[d], (g, ahead[d], m))
    for d in (1, 2, 3):
        go(meta.at[0], meta.at[d], m_send.at[d], m_recv.at[d], (g, ahead[d], m))
    for d in (1, 3, 2):
        mine = gathered.at[block(d), cols(m)]
        send(mine, mine, z_send.at[d], z_recv.at[d], (g, ahead[d], m)).wait_recv()
        for j in (3, 1, 2):
            go(mine, mine, f_send.at[d, j], f_recv.at[d, j], (g, e, mp_peer[j]))
    for d in (1, 2, 3):
        send(meta.at[d], meta.at[d], m_send.at[d], m_recv.at[d], (g, ahead[d], m)).wait_recv()
    for d in (1, 3, 2):
        for j in (1, 2, 3):
            theirs = gathered.at[block(d), cols(mp_peer[j])]
            send(theirs, theirs, f_send.at[d, j], f_recv.at[d, j], (g, e, mp_peer[j])).wait_recv()

    loads[0].wait()
    tile = 256

    def first(n, carry):
        at = pl.ds(pl.multiple_of(n * tile, tile), tile)
        raw = jnp.dot(gathered[...], w_in[:, at], preferred_element_type=jnp.float32)
        hidden[:, at] = jnp.maximum(raw, 0.0).astype(jnp.bfloat16)
        return carry

    lax.fori_loop(0, w_in.shape[1] // tile, first, 0)

    loads[1].wait()
    for j in (3, 1, 2, 0):
        part[j] = jnp.dot(
            hidden[...], w_out[:, cols(mp_peer[j])], preferred_element_type=jnp.float32
        ).astype(jnp.bfloat16)
        if j > 0:
            go(part.at[j], part_got.at[j], p_send.at[j], p_recv.at[j], (g, e, mp_peer[j]))
    for j in (1, 2, 3):
        send(part.at[j], part_got.at[j], p_send.at[j], p_recv.at[j], (g, e, mp_peer[j])).wait_recv()
    for d in (2, 1, 3, 0):
        at = block(d)
        whole = part[0, at, :].astype(jnp.float32)
        for j in (1, 2, 3):
            whole = whole + part_got[j, at, :].astype(jnp.float32)
        summed[at, :] = whole.astype(jnp.bfloat16)
        if d > 0:
            go(summed.at[at, :], back_got.at[d], b_send.at[d], b_recv.at[d], (g, behind[d], m))

    gates = gate_ref[0].astype(jnp.float32)
    all_gates = gates[:, 0:1] + gates[:, 1:2]
    share = (gates[:, 0:1] / all_gates, gates[:, 1:2] / all_gates)
    routes = route_ref[0]
    added = jnp.zeros((row_count, quarter), jnp.float32)
    for d in (0, 1, 3, 2):
        scale = jnp.where(routes[:, 0:1] == ahead[d], share[0], 0.0)
        scale = scale + jnp.where(routes[:, 1:2] == ahead[d], share[1], 0.0)
        if d == 0:
            came = summed[block(0), :]
        else:
            send(back_got.at[d], back_got.at[d], b_send.at[d], b_recv.at[d],
                 (g, behind[d], m)).wait_recv()
            came = back_got[d]
        added = added + scale * came.astype(jnp.float32)
    own = rows_ref[0, :, cols(m)].astype(jnp.float32) + added
    moe[:, cols(m)] = own.astype(jnp.bfloat16)
    for j in (3, 1, 2):
        go(moe.at[:, cols(m)], moe.at[:, cols(m)], e_send.at[j], e_recv.at[j], (g, e, mp_peer[j]))
    for j in (1, 2, 3):
        theirs = moe.at[:, cols(mp_peer[j])]
        send(theirs, theirs, e_send.at[j], e_recv.at[j], (g, e, mp_peer[j])).wait_recv()
    loads[2].wait()
    loads[3].wait()
    moe_ref[0] = moe[...]
    encoded = norm_rows(moe[...].astype(jnp.float32), attn_gain_ref[...])

    def kv_copy(d, group, place):
        return send(kv, kv_got.at[block(d), :], k_send.at[d], k_recv.at[d], (group, place, m))

    @pl.when(g == 0)
    def _():
        kv[...] = jnp.dot(encoded, attn[...], preferred_element_type=jnp.float32).astype(
            jnp.bfloat16
        )
        for d in (2, 1, 3, 0):
            kv_copy(d, 1, ahead[d]).start()
        step_ref[0] = encoded
        for d in range(n_expert):
            kv_copy(d, 1, ahead[d]).wait_send()

    @pl.when(g == 1)
    def _():
        query = jnp.dot(
            encoded, attn[:, 0:head_width], preferred_element_type=jnp.float32
        ).astype(jnp.bfloat16)
        positions = cache.shape[0] // row_count
        lane = lax.broadcasted_iota(jnp.int32, (1, total), 1).astype(jnp.float32)
        slot = lax.broadcasted_iota(jnp.int32, (row_count, 1), 0).astype(jnp.float32)
        square = (row_count, row_count)
        diagonal = lax.broadcasted_iota(jnp.int32, square, 0) == lax.broadcasted_iota(
            jnp.int32, square, 1
        )
        lengths = jnp.sum(
            jnp.where(diagonal, cache_len_ref[...].astype(jnp.float32), 0.0), axis=1, keepdims=True
        )
        cell = jnp.full((1, total), -1.0, jnp.float32)
        first_slot = (e * row_count).astype(jnp.float32)
        for d in range(n_expert):
            facts = meta[d].astype(jnp.float32)
            start = jnp.full((1, 1), float(d * row_count), jnp.float32)
            for s in range(src_ref.shape[1]):
                length = facts[0:1, s : s + 1]
                place = facts[1:2, s : s + 1] - first_slot
                here = (lane >= start) & (lane < start + length)
                cell = jnp.where(here, place * positions + lane - start, cell)
                lengths = jnp.where(slot == place, length, lengths)
                start = start + length
        cell = cell.astype(jnp.int32)
        for d in range(n_expert):
            kv_copy(d, 1, ahead[d]).wait_recv()

        def place_cells(c, carry):
            at = pl.ds(pl.multiple_of(c * tile, tile), tile)
            spot = lax.broadcasted_iota(jnp.int32, (tile, total), 0) + c * tile
            hit = jnp.where(spot == cell, 1.0, 0.0)
            kept = 1.0 - jnp.sum(hit, axis=1, keepdims=True)
            new = jnp.dot(hit.astype(jnp.bfloat16), kv_got[...], preferred_element_type=jnp.float32)
            slot_kv[at, :] = (new + kept * cache[at, :].astype(jnp.float32)).astype(jnp.bfloat16)
            return carry

        lax.fori_loop(0, cache.shape[0] // tile, place_cells, 0)
        shape = (row_count, cache.shape[0])
        spot = lax.broadcasted_iota(jnp.int32, shape, 1)
        offset = spot - positions * lax.broadcasted_iota(jnp.int32, shape, 0)
        inside = (offset >= 0) & (offset < lengths.astype(jnp.int32))
        pieces = []
        for h in range(head_width // HEAD_DIM):
            low, high = h * HEAD_DIM, (h + 1) * HEAD_DIM
            scores = lax.dot_general(
                query[:, low:high], slot_kv[:, low:high], NT, preferred_element_type=jnp.float32
            ) * (1.0 / math.sqrt(HEAD_DIM))
            scores = jnp.where(inside, scores, -1e30)
            highest = jnp.max(scores, axis=-1, keepdims=True)
            raised = jnp.where(inside, jnp.exp(scores - highest), 0.0)
            probs = (raised / jnp.sum(raised, axis=-1, keepdims=True)).astype(jnp.bfloat16)
            pieces.append(
                jnp.dot(
                    probs,
                    slot_kv[:, head_width + low : head_width + high],
                    preferred_element_type=jnp.float32,
                ).astype(jnp.bfloat16)
            )
        context = jnp.concatenate(pieces, axis=1)

        def mixed_copy(j):
            return send(mixed.at[j], mixed_got.at[j], g_send.at[j], g_recv.at[j],
                        (g, e, mp_peer[j]))

        def final_copy(j, place):
            return send(final.at[:, cols(place)], final.at[:, cols(place)], h_send.at[j],
                        h_recv.at[j], (g, e, mp_peer[j]))

        for j in (3, 1, 2, 0):
            mixed[j] = lax.dot_general(
                context, attn[cols(mp_peer[j]), head_width : 2 * head_width], NT,
                preferred_element_type=jnp.float32,
            ).astype(jnp.bfloat16)
            if j > 0:
                mixed_copy(j).start()
        out = mixed[0].astype(jnp.float32)
        for j in (1, 2, 3):
            mixed_copy(j).wait_recv()
            out = out + mixed_got[j].astype(jnp.float32)
        out = out + moe[:, cols(m)].astype(jnp.float32)
        final[:, cols(m)] = out.astype(jnp.bfloat16)
        for j in (3, 1, 2):
            final_copy(j, m).start()
        for j in (1, 2, 3):
            final_copy(j, mp_peer[j]).wait_recv()
        step_ref[0] = final[...]
        for j in (1, 2, 3):
            mixed_copy(j).wait_send()
            final_copy(j, m).wait_send()

    for copy in pending:
        copy.wait_send()


def dense_body(
    rows, route, gate_int, moe_gain, w_in, w_out, attn_gain, attn_weight, src_len, target, cache,
    cache_len,
):
    row_count, width = rows.shape[1], rows.shape[2]
    n_expert = lax.axis_size("expert")
    total = n_expert * row_count
    units = w_in.shape[3]
    quarter = width // 4
    attn = attn_weight[0].reshape(width, -1)
    kv_cache = cache.reshape(row_count * cache.shape[1], -1)
    both = attn.shape[1]
    bf16 = jnp.bfloat16
    dma = pltpu.SemaphoreType.DMA
    vmem = pl.BlockSpec(memory_space=pltpu.VMEM)
    hbm = pl.BlockSpec(memory_space=pl.ANY)
    flops = 4 * total * width * units
    return pl.pallas_call(
        kernel,
        out_shape=(jax.ShapeDtypeStruct(rows.shape, bf16), jax.ShapeDtypeStruct(rows.shape, bf16)),
        in_specs=[vmem] * 8 + [hbm] * 4,
        out_specs=(vmem, vmem),
        scratch_shapes=[
            pltpu.VMEM((width, units), bf16),
            pltpu.VMEM((units, width), bf16),
            pltpu.VMEM(attn.shape, bf16),
            pltpu.VMEM(kv_cache.shape, bf16),
            pltpu.VMEM((total, width), bf16),
            pltpu.VMEM((total, units), bf16),
            pltpu.VMEM((4, total, quarter), bf16),
            pltpu.VMEM((4, total, quarter), bf16),
            pltpu.VMEM((total, quarter), bf16),
            pltpu.VMEM((n_expert, row_count, quarter), bf16),
            pltpu.VMEM((row_count, width), bf16),
            pltpu.VMEM((n_expert, 8, 128), jnp.int32),
            pltpu.VMEM((row_count, both), bf16),
            pltpu.VMEM((total, both), bf16),
            pltpu.VMEM(kv_cache.shape, bf16),
            pltpu.VMEM((4, row_count, quarter), bf16),
            pltpu.VMEM((4, row_count, quarter), bf16),
            pltpu.VMEM((row_count, width), bf16),
            dma((4,)),
            dma((n_expert,)), dma((n_expert,)),
            dma((n_expert,)), dma((n_expert,)),
            dma((n_expert, 4)), dma((n_expert, 4)),
            dma((4,)), dma((4,)),
            dma((n_expert,)), dma((n_expert,)),
            dma((4,)), dma((4,)),
            dma((n_expert,)), dma((n_expert,)),
            dma((4,)), dma((4,)),
            dma((4,)), dma((4,)),
        ],
        compiler_params=pltpu.CompilerParams(
            collective_id=0, has_side_effects=True, vmem_limit_bytes=48 * 1024 * 1024
        ),
        cost_estimate=pl.CostEstimate(flops=flops, bytes_accessed=12 << 20, transcendentals=0),
    )(
        rows, route, gate_int, moe_gain, attn_gain, src_len, target, cache_len.reshape(1, -1),
        w_in, w_out, attn, kv_cache,
    )


def solution(mesh):
    dense = mesh.shape["expert"] == 4 and mesh.shape["mp"] == 4
    return jax.shard_map(
        dense_body if dense else spread_body,
        mesh=mesh,
        in_specs=(
            P("group", "expert", None),
            P("group", "expert", None),
            P("group", "expert", None),
            P("group", None),
            P("group", "expert", None, "mp"),
            P("group", "expert", "mp", None),
            P("group", None),
            P("group", None, None, "mp"),
            P("expert", None),
            P("expert", None),
            P("expert", None, None, "mp"),
            P("expert"),
        ),
        out_specs=(P("group", "expert", None), P("group", "expert", None)),
        check_vma=False,
    )
```

```python
import math

import jax
import jax.numpy as jnp
from jax import lax
from jax.experimental import pallas as pl
from jax.experimental.pallas import tpu as pltpu
from jax.sharding import PartitionSpec as P

HEAD_DIM = 128


def layer_norm(values, gain):
    center = values - jnp.mean(values, axis=-1, keepdims=True)
    spread = jnp.mean(center * center, axis=-1, keepdims=True)
    return center * lax.rsqrt(spread + 1e-05) * gain


def spread_body(
    rows,
    route,
    gate_int,
    moe_gain,
    w_in,
    w_out,
    attn_gain,
    attn_weight,
    src_len,
    target,
    cache,
    cache_len,
):
    experts_count = lax.axis_size("expert")
    row_count = rows.shape[1]
    width = rows.shape[2]
    group_place = lax.axis_index("group")
    expert_place = lax.axis_index("expert")
    capacity = max(2, 4 * row_count // experts_count)
    base = rows[0].astype(jnp.float32)
    normed = layer_norm(base, moe_gain[0]).astype(jnp.bfloat16)
    weights = gate_int[0].astype(jnp.float32)
    weights = weights / jnp.sum(weights, axis=1, keepdims=True)
    flat_dest = route[0].reshape(-1)
    onehot = (flat_dest[:, None] == jnp.arange(experts_count)[None, :]).astype(jnp.int32)
    position = jnp.sum((jnp.cumsum(onehot, axis=0) - 1) * onehot, axis=1)
    flat_index = flat_dest * capacity + position
    pair_index = flat_index.reshape(row_count, 2)
    slot_iota = jnp.arange(experts_count * capacity, dtype=jnp.int32)
    slot_table = (
        (slot_iota[:, None] == pair_index[None, :, 0])
        | (slot_iota[:, None] == pair_index[None, :, 1])
    ).astype(jnp.bfloat16)
    buffer = jnp.dot(slot_table, normed, preferred_element_type=jnp.float32).astype(jnp.bfloat16)
    buffer = buffer.reshape(experts_count, capacity, normed.shape[1])
    hidden = jax.nn.relu(
        jnp.einsum(
            "sci,if->scf",
            lax.all_to_all(buffer, "expert", split_axis=0, concat_axis=0, tiled=True),
            w_in[0, 0],
            preferred_element_type=jnp.float32,
        )
    ).astype(jnp.bfloat16)
    partial_rows = jnp.einsum(
        "scf,fo->sco", hidden, w_out[0, 0], preferred_element_type=jnp.float32
    )
    summed = lax.psum(partial_rows.astype(jnp.bfloat16), "mp")
    returned = lax.all_to_all(summed, "expert", split_axis=0, concat_axis=0, tiled=True)
    returned = returned.reshape(experts_count * capacity, returned.shape[2])
    picked = returned[flat_index].reshape(row_count, 2, returned.shape[1]).astype(jnp.float32)
    added = weights[:, 0:1] * picked[:, 0] + weights[:, 1:2] * picked[:, 1]
    moe_rows = (base + added).astype(jnp.bfloat16)
    encoded = layer_norm(moe_rows.astype(jnp.float32), attn_gain[0]).astype(jnp.bfloat16)
    head_width = attn_weight.shape[3]
    projected = jnp.dot(
        encoded, attn_weight[0].reshape(width, 2 * head_width), preferred_element_type=jnp.float32
    )
    projected = projected.reshape(row_count, 2, head_width).astype(jnp.bfloat16)
    query = projected[:, 0, :]
    lengths = src_len[0]
    ends = jnp.cumsum(lengths)
    starts = ends - lengths
    row_iota = jnp.arange(row_count, dtype=jnp.int32)
    which = jnp.sum((row_iota[:, None] >= ends[None, :]).astype(jnp.int32), axis=1)
    select = which[:, None] == jnp.arange(lengths.shape[0])[None, :]
    row_start = jnp.sum(jnp.where(select, starts[None, :], 0), axis=1)
    row_len = jnp.sum(jnp.where(select, lengths[None, :], 0), axis=1)
    row_slot = jnp.sum(jnp.where(select, target[0][None, :], 0), axis=1)
    row_pos = row_iota - row_start
    positions = cache.shape[1]
    cell_iota = jnp.arange(row_count * positions, dtype=jnp.int32)
    slot_ids = jnp.arange(row_count, dtype=jnp.int32)
    sent_slot = jnp.where(group_place == 0, row_slot, -1)
    slot_kv = cache
    slot_len = cache_len
    kv_piece = lax.all_gather(projected, ("group", "expert"), axis=0, tiled=True)
    slot_piece = lax.all_gather(sent_slot, ("group", "expert"), axis=0, tiled=True)
    pos_piece = lax.all_gather(row_pos, ("group", "expert"), axis=0, tiled=True)
    len_piece = lax.all_gather(row_len, ("group", "expert"), axis=0, tiled=True)
    local = slot_piece - expert_place * row_count
    inside = (local >= 0) & (local < row_count)
    cell = jnp.where(inside, local * positions + pos_piece, -1)
    hit = cell_iota[:, None] == cell[None, :]
    written = jnp.dot(
        hit.astype(jnp.bfloat16),
        kv_piece.reshape(kv_piece.shape[0], -1),
        preferred_element_type=jnp.float32,
    )
    written = written.astype(jnp.bfloat16).reshape(slot_kv.shape)
    touched = jnp.any(hit, axis=1).reshape(row_count, positions)
    slot_kv = jnp.where(touched[:, :, None, None], written, slot_kv)
    slot_hit = (slot_ids[:, None] == local[None, :]) & inside[None, :]
    fresh = jnp.max(jnp.where(slot_hit, len_piece[None, :], 0), axis=1).astype(jnp.int32)
    slot_len = jnp.where(jnp.any(slot_hit, axis=1), fresh, slot_len)
    slot_kv, slot_len = (slot_kv, slot_len)
    heads_here = head_width // HEAD_DIM
    keys = slot_kv[:, :, 0, :].reshape(row_count, positions, heads_here, HEAD_DIM)
    values = slot_kv[:, :, 1, :].reshape(row_count, positions, heads_here, HEAD_DIM)
    heads_query = query.reshape(row_count, heads_here, HEAD_DIM)
    scores = jnp.einsum("thd,tphd->thp", heads_query, keys, preferred_element_type=jnp.float32) * (
        1.0 / math.sqrt(HEAD_DIM)
    )
    inside = jnp.arange(positions)[None, None, :] < slot_len[:, None, None]
    scores = jnp.where(inside, scores, -1e30)
    highest = jnp.max(scores, axis=-1, keepdims=True)
    raised = jnp.where(inside, jnp.exp(scores - highest), 0.0)
    probs = (raised / jnp.sum(raised, axis=-1, keepdims=True)).astype(jnp.bfloat16)
    context = jnp.einsum("thp,tphd->thd", probs, values, preferred_element_type=jnp.float32).astype(
        jnp.bfloat16
    )
    context = context.reshape(row_count, head_width)
    output_map = attn_weight[0][:, 1, :]
    mixed = lax.dot_general(
        context, output_map, (((1,), (1,)), ((), ())), preferred_element_type=jnp.float32
    )
    mixed = lax.psum(mixed.astype(jnp.bfloat16), "mp").astype(jnp.float32)
    decoded = (moe_rows.astype(jnp.float32) + mixed).astype(jnp.bfloat16)
    step_rows = jnp.where(group_place == 0, encoded, decoded)
    return (moe_rows[None], step_rows[None])


MESH = pl.DeviceIdType.MESH
NT = (((1,), (1,)), ((), ()))


def norm_rows(values, gain):
    center = values - jnp.mean(values, axis=-1, keepdims=True)
    spread = jnp.mean(center * center, axis=-1, keepdims=True)
    return (center * lax.rsqrt(spread + 1e-05) * gain).astype(jnp.bfloat16)


def kernel(
    rows_ref, route_ref, gate_ref, moe_gain_ref, attn_gain_ref, src_ref, target_ref, cache_len_ref,
    attn, cache, w_in_hbm, w_out_hbm,
    moe_ref, step_ref,
    w_in, w_out, gathered, hidden, part, part_got, summed, back_got, moe, meta,
    kv, kv_got, mixed, mixed_got, final,
    load_sem, z_send, z_recv, m_send, m_recv, f_send, f_recv, p_send, p_recv, b_send, b_recv,
    e_send, e_recv, k_send, k_recv, g_send, g_recv, h_send, h_recv,
):
    g = lax.axis_index("group")
    e = lax.axis_index("expert")
    m = lax.axis_index("mp")
    n_expert = lax.axis_size("expert")
    row_count = rows_ref.shape[1]
    width = rows_ref.shape[2]
    quarter = width // 4
    head_width = attn.shape[1] // 2
    total = n_expert * row_count
    y, x = m // 2, m % 2
    mp_peer = (m, y * 2 + 1 - x, (1 - y) * 2 + x, 3 - m)
    ahead = [(e + d) % n_expert for d in range(n_expert)]
    behind = [(e + n_expert - d) % n_expert for d in range(n_expert)]

    loads = [
        pltpu.make_async_copy(w_in_hbm.at[0, 0], w_in, load_sem.at[0]),
        pltpu.make_async_copy(w_out_hbm.at[0, 0], w_out, load_sem.at[1]),
    ]
    barrier = pltpu.get_barrier_semaphore()
    friends = [(g, ahead[d], m) for d in range(1, n_expert)]
    friends += [(g, e, mp_peer[j]) for j in (1, 2, 3)]
    friends += [(1 - g, ahead[d], m) for d in range(n_expert)]
    for friend in friends:
        pl.semaphore_signal(barrier, inc=1, device_id=friend, device_id_type=MESH)
    for load in loads:
        load.start()

    def cols(place):
        return pl.ds(pl.multiple_of(place * quarter, quarter), quarter)

    order = (0, 1, 3, 2)
    spans = ((0, 1), (1, 3), (3, 4))

    def block(d):
        return pl.ds(order.index(d) * row_count, row_count)

    def kv_block(d):
        return pl.ds(d * row_count, row_count)

    def span(k):
        low, high = spans[k]
        return pl.ds(low * row_count, (high - low) * row_count)

    def send(src, dst, send_sem, recv_sem, device):
        copy = pltpu.make_async_remote_copy(
            src_ref=src, dst_ref=dst, send_sem=send_sem, recv_sem=recv_sem,
            device_id=device, device_id_type=MESH,
        )
        return copy

    pending = []

    def go(*args):
        copy = send(*args)
        copy.start()
        pending.append(copy)

    base = rows_ref[0].astype(jnp.float32)
    gathered[block(0), :] = norm_rows(base, moe_gain_ref[...])
    meta[0] = jnp.zeros(meta.shape[1:], jnp.int32)
    meta[0, 0:1, 0:src_ref.shape[1]] = src_ref[...]
    meta[0, 1:2, 0:src_ref.shape[1]] = target_ref[...]
    pl.semaphore_wait(barrier, len(friends))

    def z_copy(d):
        return send(gathered.at[block(0), cols(m)], gathered.at[block(d), cols(m)],
                    z_send.at[d], z_recv.at[d], (g, ahead[d], m))

    def forward(d):
        mine = gathered.at[block(d), cols(m)]
        z_copy(d).wait_recv()
        for j in (3, 1, 2):
            go(mine, mine, f_send.at[d, j], f_recv.at[d, j], (g, e, mp_peer[j]))

    def forwarded(d):
        for j in (1, 2, 3):
            theirs = gathered.at[block(d), cols(mp_peer[j])]
            send(theirs, theirs, f_send.at[d, j], f_recv.at[d, j], (g, e, mp_peer[j])).wait_recv()

    tile = 256

    def first_product(k):
        def step(n, carry):
            at = pl.ds(pl.multiple_of(n * tile, tile), tile)
            raw = jnp.dot(gathered[span(k), :], w_in[:, at], preferred_element_type=jnp.float32)
            hidden[span(k), at] = jnp.maximum(raw, 0.0).astype(jnp.bfloat16)
            return carry

        lax.fori_loop(0, w_in.shape[1] // tile, step, 0)

    def part_copy(k, j):
        return send(part.at[j, span(k), :], part_got.at[j, span(k), :], p_send.at[k, j],
                    p_recv.at[k, j], (g, e, mp_peer[j]))

    def second_product(k):
        for j in (3, 1, 2, 0):
            part[j, span(k), :] = jnp.dot(
                hidden[span(k), :], w_out[:, cols(mp_peer[j])], preferred_element_type=jnp.float32
            ).astype(jnp.bfloat16)
            if j > 0:
                pending.append(part_copy(k, j))
                pending[-1].start()

    def add_parts(k):
        for j in (1, 2, 3):
            part_copy(k, j).wait_recv()
        for d in order[spans[k][0] : spans[k][1]]:
            at = block(d)
            whole = part[0, at, :].astype(jnp.float32)
            for j in (1, 2, 3):
                whole = whole + part_got[j, at, :].astype(jnp.float32)
            summed[at, :] = whole.astype(jnp.bfloat16)
            if d > 0:
                go(summed.at[at, :], back_got.at[d], b_send.at[d], b_recv.at[d], (g, behind[d], m))

    for d in (1, 3, 2):
        pending.append(z_copy(d))
        pending[-1].start()
    for d in (1, 2, 3):
        go(meta.at[0], meta.at[d], m_send.at[d], m_recv.at[d], (g, ahead[d], m))
    loads[0].wait()
    first_product(0)
    forward(1)
    forward(3)
    loads[1].wait()
    second_product(0)
    forward(2)
    forwarded(1)
    forwarded(3)
    first_product(1)
    second_product(1)
    forwarded(2)
    first_product(2)
    second_product(2)
    add_parts(0)
    add_parts(1)
    add_parts(2)

    square = (row_count, row_count)
    diagonal = lax.broadcasted_iota(jnp.int32, square, 0) == lax.broadcasted_iota(
        jnp.int32, square, 1
    )

    def upright(line):
        return jnp.sum(jnp.where(diagonal, line.astype(jnp.float32), 0.0), axis=1, keepdims=True)

    gates = [upright(gate_ref[0, k : k + 1, :]) for k in (0, 1)]
    routes = [upright(route_ref[0, k : k + 1, :]) for k in (0, 1)]
    share = [gate / (gates[0] + gates[1]) for gate in gates]
    for d in (1, 2, 3):
        send(meta.at[d], meta.at[d], m_send.at[d], m_recv.at[d], (g, ahead[d], m)).wait_recv()
    added = jnp.zeros((row_count, quarter), jnp.float32)
    for d in (0, 1, 3, 2):
        expert = ahead[d].astype(jnp.float32)
        scale = jnp.where(routes[0] == expert, share[0], 0.0)
        scale = scale + jnp.where(routes[1] == expert, share[1], 0.0)
        if d == 0:
            came = summed[block(0), :]
        else:
            send(back_got.at[d], back_got.at[d], b_send.at[d], b_recv.at[d],
                 (g, behind[d], m)).wait_recv()
            came = back_got[d]
        added = added + scale * came.astype(jnp.float32)
    own = rows_ref[0, :, cols(m)].astype(jnp.float32) + added
    moe[:, cols(m)] = own.astype(jnp.bfloat16)
    for j in (3, 1, 2):
        go(moe.at[:, cols(m)], moe.at[:, cols(m)], e_send.at[j], e_recv.at[j], (g, e, mp_peer[j]))
    for j in (1, 2, 3):
        theirs = moe.at[:, cols(mp_peer[j])]
        send(theirs, theirs, e_send.at[j], e_recv.at[j], (g, e, mp_peer[j])).wait_recv()
    moe_ref[0] = moe[...]
    encoded = norm_rows(moe[...].astype(jnp.float32), attn_gain_ref[...])

    def kv_copy(d, group, place):
        return send(kv, kv_got.at[kv_block(d), :], k_send.at[d], k_recv.at[d], (group, place, m))

    @pl.when(g == 0)
    def _():
        kv[...] = jnp.dot(encoded, attn[...], preferred_element_type=jnp.float32).astype(
            jnp.bfloat16
        )
        for d in (2, 1, 3, 0):
            kv_copy(d, 1, ahead[d]).start()
        step_ref[0] = encoded
        for d in range(n_expert):
            kv_copy(d, 1, ahead[d]).wait_send()

    @pl.when(g == 1)
    def _():
        query = jnp.dot(
            encoded, attn[:, 0:head_width], preferred_element_type=jnp.float32
        ).astype(jnp.bfloat16)
        positions = cache.shape[0] // row_count
        lane = lax.broadcasted_iota(jnp.int32, (1, total), 1).astype(jnp.float32)
        slot = lax.broadcasted_iota(jnp.int32, (row_count, 1), 0).astype(jnp.float32)
        lengths = upright(cache_len_ref[...])
        row_slot = jnp.full((1, total), -1.0, jnp.float32)
        first_slot = (e * row_count).astype(jnp.float32)
        for d in range(n_expert):
            facts = meta[d].astype(jnp.float32)
            start = jnp.full((1, 1), float(d * row_count), jnp.float32)
            for s in range(src_ref.shape[1]):
                length = facts[0:1, s : s + 1]
                place = facts[1:2, s : s + 1] - first_slot
                here = (lane >= start) & (lane < start + length)
                row_slot = jnp.where(here, place, row_slot)
                lengths = jnp.where(slot == place, 0.0, lengths)
                start = start + length
        shape = (row_count, cache.shape[0])
        offset = lax.broadcasted_iota(
            jnp.int32, shape, 1
        ) - positions * lax.broadcasted_iota(jnp.int32, shape, 0)
        held = (offset >= 0) & (offset < lengths.astype(jnp.int32))
        fresh = slot == row_slot

        def attend(h, pool, inside):
            low, high = h * HEAD_DIM, (h + 1) * HEAD_DIM
            scores = lax.dot_general(
                query[:, low:high], pool[:, low:high], NT, preferred_element_type=jnp.float32
            ) * (1.0 / math.sqrt(HEAD_DIM))
            scores = jnp.where(inside, scores, -1e30)
            highest = jnp.max(scores, axis=-1, keepdims=True)
            raised = jnp.where(inside, jnp.exp(scores - highest), 0.0)
            weight = jnp.sum(raised, axis=-1, keepdims=True)
            probs = (raised / jnp.where(weight > 0.0, weight, 1.0)).astype(jnp.bfloat16)
            return jnp.dot(
                probs, pool[:, head_width + low : head_width + high],
                preferred_element_type=jnp.float32,
            )

        heads = range(head_width // HEAD_DIM)
        from_cache = [attend(h, cache, held) for h in heads]
        for d in range(n_expert):
            kv_copy(d, 1, ahead[d]).wait_recv()
        pieces = [(from_cache[h] + attend(h, kv_got, fresh)).astype(jnp.bfloat16) for h in heads]
        context = jnp.concatenate(pieces, axis=1)

        def mixed_copy(j):
            return send(mixed.at[j], mixed_got.at[j], g_send.at[j], g_recv.at[j],
                        (g, e, mp_peer[j]))

        def final_copy(j, place):
            return send(final.at[:, cols(place)], final.at[:, cols(place)], h_send.at[j],
                        h_recv.at[j], (g, e, mp_peer[j]))

        for j in (3, 1, 2, 0):
            mixed[j] = lax.dot_general(
                context, attn[cols(mp_peer[j]), head_width : 2 * head_width], NT,
                preferred_element_type=jnp.float32,
            ).astype(jnp.bfloat16)
            if j > 0:
                mixed_copy(j).start()
        out = mixed[0].astype(jnp.float32)
        for j in (1, 2, 3):
            mixed_copy(j).wait_recv()
            out = out + mixed_got[j].astype(jnp.float32)
        out = out + moe[:, cols(m)].astype(jnp.float32)
        final[:, cols(m)] = out.astype(jnp.bfloat16)
        for j in (3, 1, 2):
            final_copy(j, m).start()
        for j in (1, 2, 3):
            final_copy(j, mp_peer[j]).wait_recv()
        step_ref[0] = final[...]
        for j in (1, 2, 3):
            mixed_copy(j).wait_send()
            final_copy(j, m).wait_send()

    for copy in pending:
        copy.wait_send()


def dense_body(
    rows, route, gate_int, moe_gain, w_in, w_out, attn_gain, attn_weight, src_len, target, cache,
    cache_len,
):
    row_count, width = rows.shape[1], rows.shape[2]
    n_expert = lax.axis_size("expert")
    total = n_expert * row_count
    units = w_in.shape[3]
    quarter = width // 4
    attn = attn_weight[0].reshape(width, -1)
    kv_cache = cache.reshape(row_count * cache.shape[1], -1)
    both = attn.shape[1]
    bf16 = jnp.bfloat16
    dma = pltpu.SemaphoreType.DMA
    vmem = pl.BlockSpec(memory_space=pltpu.VMEM)
    hbm = pl.BlockSpec(memory_space=pl.ANY)
    flops = 4 * total * width * units
    return pl.pallas_call(
        kernel,
        out_shape=(jax.ShapeDtypeStruct(rows.shape, bf16), jax.ShapeDtypeStruct(rows.shape, bf16)),
        in_specs=[vmem] * 10 + [hbm] * 2,
        out_specs=(vmem, vmem),
        scratch_shapes=[
            pltpu.VMEM((width, units), bf16),
            pltpu.VMEM((units, width), bf16),
            pltpu.VMEM((total, width), bf16),
            pltpu.VMEM((total, units), bf16),
            pltpu.VMEM((4, total, quarter), bf16),
            pltpu.VMEM((4, total, quarter), bf16),
            pltpu.VMEM((total, quarter), bf16),
            pltpu.VMEM((n_expert, row_count, quarter), bf16),
            pltpu.VMEM((row_count, width), bf16),
            pltpu.VMEM((n_expert, 8, 128), jnp.int32),
            pltpu.VMEM((row_count, both), bf16),
            pltpu.VMEM((total, both), bf16),
            pltpu.VMEM((4, row_count, quarter), bf16),
            pltpu.VMEM((4, row_count, quarter), bf16),
            pltpu.VMEM((row_count, width), bf16),
            dma((2,)),
            dma((n_expert,)), dma((n_expert,)),
            dma((n_expert,)), dma((n_expert,)),
            dma((n_expert, 4)), dma((n_expert, 4)),
            dma((3, 4)), dma((3, 4)),
            dma((n_expert,)), dma((n_expert,)),
            dma((4,)), dma((4,)),
            dma((n_expert,)), dma((n_expert,)),
            dma((4,)), dma((4,)),
            dma((4,)), dma((4,)),
        ],
        compiler_params=pltpu.CompilerParams(
            collective_id=0, has_side_effects=True, vmem_limit_bytes=48 * 1024 * 1024
        ),
        cost_estimate=pl.CostEstimate(flops=flops, bytes_accessed=12 << 20, transcendentals=0),
    )(
        rows, route.transpose(0, 2, 1), gate_int.transpose(0, 2, 1), moe_gain, attn_gain, src_len,
        target, cache_len.reshape(1, -1), attn, kv_cache, w_in, w_out,
    )


def solution(mesh):
    dense = mesh.shape["expert"] == 4 and mesh.shape["mp"] == 4
    return jax.shard_map(
        dense_body if dense else spread_body,
        mesh=mesh,
        in_specs=(
            P("group", "expert", None),
            P("group", "expert", None),
            P("group", "expert", None),
            P("group", None),
            P("group", "expert", None, "mp"),
            P("group", "expert", "mp", None),
            P("group", None),
            P("group", None, None, "mp"),
            P("expert", None),
            P("expert", None),
            P("expert", None, None, "mp"),
            P("expert"),
        ),
        out_specs=(P("group", "expert", None), P("group", "expert", None)),
        check_vma=False,
    )
```

```python
import math

import jax
import jax.numpy as jnp
from jax import lax
from jax.experimental import pallas as pl
from jax.experimental.pallas import tpu as pltpu
from jax.sharding import PartitionSpec as P

HEAD_DIM = 128


def layer_norm(values, gain):
    center = values - jnp.mean(values, axis=-1, keepdims=True)
    spread = jnp.mean(center * center, axis=-1, keepdims=True)
    return center * lax.rsqrt(spread + 1e-05) * gain


def spread_body(
    rows,
    route,
    gate_int,
    moe_gain,
    w_in,
    w_out,
    attn_gain,
    attn_weight,
    src_len,
    target,
    cache,
    cache_len,
):
    experts_count = lax.axis_size("expert")
    row_count = rows.shape[1]
    width = rows.shape[2]
    group_place = lax.axis_index("group")
    expert_place = lax.axis_index("expert")
    capacity = max(2, 4 * row_count // experts_count)
    base = rows[0].astype(jnp.float32)
    normed = layer_norm(base, moe_gain[0]).astype(jnp.bfloat16)
    weights = gate_int[0].astype(jnp.float32)
    weights = weights / jnp.sum(weights, axis=1, keepdims=True)
    flat_dest = route[0].reshape(-1)
    onehot = (flat_dest[:, None] == jnp.arange(experts_count)[None, :]).astype(jnp.int32)
    position = jnp.sum((jnp.cumsum(onehot, axis=0) - 1) * onehot, axis=1)
    flat_index = flat_dest * capacity + position
    pair_index = flat_index.reshape(row_count, 2)
    slot_iota = jnp.arange(experts_count * capacity, dtype=jnp.int32)
    slot_table = (
        (slot_iota[:, None] == pair_index[None, :, 0])
        | (slot_iota[:, None] == pair_index[None, :, 1])
    ).astype(jnp.bfloat16)
    buffer = jnp.dot(slot_table, normed, preferred_element_type=jnp.float32).astype(jnp.bfloat16)
    buffer = buffer.reshape(experts_count, capacity, normed.shape[1])
    hidden = jax.nn.relu(
        jnp.einsum(
            "sci,if->scf",
            lax.all_to_all(buffer, "expert", split_axis=0, concat_axis=0, tiled=True),
            w_in[0, 0],
            preferred_element_type=jnp.float32,
        )
    ).astype(jnp.bfloat16)
    partial_rows = jnp.einsum(
        "scf,fo->sco", hidden, w_out[0, 0], preferred_element_type=jnp.float32
    )
    summed = lax.psum(partial_rows.astype(jnp.bfloat16), "mp")
    returned = lax.all_to_all(summed, "expert", split_axis=0, concat_axis=0, tiled=True)
    returned = returned.reshape(experts_count * capacity, returned.shape[2])
    picked = returned[flat_index].reshape(row_count, 2, returned.shape[1]).astype(jnp.float32)
    added = weights[:, 0:1] * picked[:, 0] + weights[:, 1:2] * picked[:, 1]
    moe_rows = (base + added).astype(jnp.bfloat16)
    encoded = layer_norm(moe_rows.astype(jnp.float32), attn_gain[0]).astype(jnp.bfloat16)
    head_width = attn_weight.shape[3]
    projected = jnp.dot(
        encoded, attn_weight[0].reshape(width, 2 * head_width), preferred_element_type=jnp.float32
    )
    projected = projected.reshape(row_count, 2, head_width).astype(jnp.bfloat16)
    query = projected[:, 0, :]
    lengths = src_len[0]
    ends = jnp.cumsum(lengths)
    starts = ends - lengths
    row_iota = jnp.arange(row_count, dtype=jnp.int32)
    which = jnp.sum((row_iota[:, None] >= ends[None, :]).astype(jnp.int32), axis=1)
    select = which[:, None] == jnp.arange(lengths.shape[0])[None, :]
    row_start = jnp.sum(jnp.where(select, starts[None, :], 0), axis=1)
    row_len = jnp.sum(jnp.where(select, lengths[None, :], 0), axis=1)
    row_slot = jnp.sum(jnp.where(select, target[0][None, :], 0), axis=1)
    row_pos = row_iota - row_start
    positions = cache.shape[1]
    cell_iota = jnp.arange(row_count * positions, dtype=jnp.int32)
    slot_ids = jnp.arange(row_count, dtype=jnp.int32)
    sent_slot = jnp.where(group_place == 0, row_slot, -1)
    slot_kv = cache
    slot_len = cache_len
    kv_piece = lax.all_gather(projected, ("group", "expert"), axis=0, tiled=True)
    slot_piece = lax.all_gather(sent_slot, ("group", "expert"), axis=0, tiled=True)
    pos_piece = lax.all_gather(row_pos, ("group", "expert"), axis=0, tiled=True)
    len_piece = lax.all_gather(row_len, ("group", "expert"), axis=0, tiled=True)
    local = slot_piece - expert_place * row_count
    inside = (local >= 0) & (local < row_count)
    cell = jnp.where(inside, local * positions + pos_piece, -1)
    hit = cell_iota[:, None] == cell[None, :]
    written = jnp.dot(
        hit.astype(jnp.bfloat16),
        kv_piece.reshape(kv_piece.shape[0], -1),
        preferred_element_type=jnp.float32,
    )
    written = written.astype(jnp.bfloat16).reshape(slot_kv.shape)
    touched = jnp.any(hit, axis=1).reshape(row_count, positions)
    slot_kv = jnp.where(touched[:, :, None, None], written, slot_kv)
    slot_hit = (slot_ids[:, None] == local[None, :]) & inside[None, :]
    fresh = jnp.max(jnp.where(slot_hit, len_piece[None, :], 0), axis=1).astype(jnp.int32)
    slot_len = jnp.where(jnp.any(slot_hit, axis=1), fresh, slot_len)
    slot_kv, slot_len = (slot_kv, slot_len)
    heads_here = head_width // HEAD_DIM
    keys = slot_kv[:, :, 0, :].reshape(row_count, positions, heads_here, HEAD_DIM)
    values = slot_kv[:, :, 1, :].reshape(row_count, positions, heads_here, HEAD_DIM)
    heads_query = query.reshape(row_count, heads_here, HEAD_DIM)
    scores = jnp.einsum("thd,tphd->thp", heads_query, keys, preferred_element_type=jnp.float32) * (
        1.0 / math.sqrt(HEAD_DIM)
    )
    inside = jnp.arange(positions)[None, None, :] < slot_len[:, None, None]
    scores = jnp.where(inside, scores, -1e30)
    highest = jnp.max(scores, axis=-1, keepdims=True)
    raised = jnp.where(inside, jnp.exp(scores - highest), 0.0)
    probs = (raised / jnp.sum(raised, axis=-1, keepdims=True)).astype(jnp.bfloat16)
    context = jnp.einsum("thp,tphd->thd", probs, values, preferred_element_type=jnp.float32).astype(
        jnp.bfloat16
    )
    context = context.reshape(row_count, head_width)
    output_map = attn_weight[0][:, 1, :]
    mixed = lax.dot_general(
        context, output_map, (((1,), (1,)), ((), ())), preferred_element_type=jnp.float32
    )
    mixed = lax.psum(mixed.astype(jnp.bfloat16), "mp").astype(jnp.float32)
    decoded = (moe_rows.astype(jnp.float32) + mixed).astype(jnp.bfloat16)
    step_rows = jnp.where(group_place == 0, encoded, decoded)
    return (moe_rows[None], step_rows[None])


MESH = pl.DeviceIdType.MESH
NT = (((1,), (1,)), ((), ()))


def norm_rows(values, gain):
    center = values - jnp.mean(values, axis=-1, keepdims=True)
    spread = jnp.mean(center * center, axis=-1, keepdims=True)
    return (center * lax.rsqrt(spread + 1e-05) * gain).astype(jnp.bfloat16)


def kernel(
    rows_ref, route_ref, gate_ref, moe_gain_ref, attn_gain_ref, src_ref, target_ref, cache_len_ref,
    w_in_hbm, w_out_hbm, attn_hbm, cache_hbm,
    moe_ref, step_ref,
    attn_pairs, cache_pairs, attn, cache, w_in, w_out, gathered, hidden, part, part_got, summed, back_got, moe, meta,
    kv, kv_got, mixed, mixed_got, final,
    load_sem, z_send, z_recv, m_send, m_recv, f_send, f_recv, p_send, p_recv, b_send, b_recv,
    e_send, e_recv, k_send, k_recv, g_send, g_recv, h_send, h_recv,
):
    g = lax.axis_index("group")
    e = lax.axis_index("expert")
    m = lax.axis_index("mp")
    n_expert = lax.axis_size("expert")
    row_count = rows_ref.shape[1]
    width = rows_ref.shape[2]
    quarter = width // 4
    head_width = attn.shape[1] // 2
    total = n_expert * row_count
    y, x = m // 2, m % 2
    mp_peer = (m, y * 2 + 1 - x, (1 - y) * 2 + x, 3 - m)
    ahead = [(e + d) % n_expert for d in range(n_expert)]
    behind = [(e + n_expert - d) % n_expert for d in range(n_expert)]

    loads = [
        pltpu.make_async_copy(w_in_hbm.at[0, 0], w_in, load_sem.at[0]),
        pltpu.make_async_copy(w_out_hbm.at[0, 0], w_out, load_sem.at[1]),
        pltpu.make_async_copy(attn_hbm, attn_pairs, load_sem.at[2]),
        pltpu.make_async_copy(cache_hbm, cache_pairs, load_sem.at[3]),
    ]
    barrier = pltpu.get_barrier_semaphore()
    friends = [(g, ahead[d], m) for d in range(1, n_expert)]
    friends += [(g, e, mp_peer[j]) for j in (1, 2, 3)]
    friends += [(1 - g, ahead[d], m) for d in range(n_expert)]
    for friend in friends:
        pl.semaphore_signal(barrier, inc=1, device_id=friend, device_id_type=MESH)
    for load in loads:
        load.start()

    def cols(place):
        return pl.ds(pl.multiple_of(place * quarter, quarter), quarter)

    order = (0, 1, 3, 2)
    spans = ((0, 1), (1, 3), (3, 4))

    def block(d):
        return pl.ds(order.index(d) * row_count, row_count)

    def kv_block(d):
        return pl.ds(d * row_count, row_count)

    def span(k):
        low, high = spans[k]
        return pl.ds(low * row_count, (high - low) * row_count)

    def send(src, dst, send_sem, recv_sem, device):
        copy = pltpu.make_async_remote_copy(
            src_ref=src, dst_ref=dst, send_sem=send_sem, recv_sem=recv_sem,
            device_id=device, device_id_type=MESH,
        )
        return copy

    pending = []

    def go(*args):
        copy = send(*args)
        copy.start()
        pending.append(copy)

    base = rows_ref[0].astype(jnp.float32)
    gathered[block(0), :] = norm_rows(base, moe_gain_ref[...])
    meta[0] = jnp.zeros(meta.shape[1:], jnp.int32)
    meta[0, 0:1, 0:src_ref.shape[1]] = src_ref[...]
    meta[0, 1:2, 0:src_ref.shape[1]] = target_ref[...]
    pl.semaphore_wait(barrier, len(friends))

    def z_copy(d):
        return send(gathered.at[block(0), cols(m)], gathered.at[block(d), cols(m)],
                    z_send.at[d], z_recv.at[d], (g, ahead[d], m))

    def forward(d):
        mine = gathered.at[block(d), cols(m)]
        z_copy(d).wait_recv()
        for j in (3, 1, 2):
            go(mine, mine, f_send.at[d, j], f_recv.at[d, j], (g, e, mp_peer[j]))

    def forwarded(d):
        for j in (1, 2, 3):
            theirs = gathered.at[block(d), cols(mp_peer[j])]
            send(theirs, theirs, f_send.at[d, j], f_recv.at[d, j], (g, e, mp_peer[j])).wait_recv()

    tile = 256

    def first_product(k):
        def step(n, carry):
            at = pl.ds(pl.multiple_of(n * tile, tile), tile)
            raw = jnp.dot(gathered[span(k), :], w_in[:, at], preferred_element_type=jnp.float32)
            hidden[span(k), at] = jnp.maximum(raw, 0.0).astype(jnp.bfloat16)
            return carry

        lax.fori_loop(0, w_in.shape[1] // tile, step, 0)

    def part_copy(k, j):
        return send(part.at[j, span(k), :], part_got.at[j, span(k), :], p_send.at[k, j],
                    p_recv.at[k, j], (g, e, mp_peer[j]))

    def second_product(k):
        for j in (3, 1, 2, 0):
            part[j, span(k), :] = jnp.dot(
                hidden[span(k), :], w_out[:, cols(mp_peer[j])], preferred_element_type=jnp.float32
            ).astype(jnp.bfloat16)
            if j > 0:
                pending.append(part_copy(k, j))
                pending[-1].start()

    def add_parts(k):
        for j in (1, 2, 3):
            part_copy(k, j).wait_recv()
        for d in order[spans[k][0] : spans[k][1]]:
            at = block(d)
            whole = part[0, at, :].astype(jnp.float32)
            for j in (1, 2, 3):
                whole = whole + part_got[j, at, :].astype(jnp.float32)
            summed[at, :] = whole.astype(jnp.bfloat16)
            if d > 0:
                go(summed.at[at, :], back_got.at[d], b_send.at[d], b_recv.at[d], (g, behind[d], m))

    def planes(pairs, flat, low, high):
        rows_at_once = 64

        def step(i, carry):
            at = pl.ds(pl.multiple_of(i * rows_at_once, rows_at_once), rows_at_once)
            for plane in (0, 1):
                flat[at, plane * head_width : (plane + 1) * head_width] = pairs[at, plane, :]
            return carry

        lax.fori_loop(low // rows_at_once, high // rows_at_once, step, 0)

    for d in (1, 3, 2):
        pending.append(z_copy(d))
        pending[-1].start()
    for d in (1, 2, 3):
        go(meta.at[0], meta.at[d], m_send.at[d], m_recv.at[d], (g, ahead[d], m))
    loads[0].wait()
    first_product(0)
    forward(1)
    forward(3)
    loads[1].wait()
    second_product(0)
    forward(2)
    loads[2].wait()
    planes(attn_pairs, attn, 0, width // 2)
    forwarded(1)
    forwarded(3)
    first_product(1)
    add_parts(0)
    second_product(1)
    forwarded(2)
    first_product(2)
    second_product(2)
    add_parts(1)
    planes(attn_pairs, attn, width // 2, 3 * width // 4)
    add_parts(2)
    planes(attn_pairs, attn, 3 * width // 4, width)

    square = (row_count, row_count)
    diagonal = lax.broadcasted_iota(jnp.int32, square, 0) == lax.broadcasted_iota(
        jnp.int32, square, 1
    )

    def upright(line):
        return jnp.sum(jnp.where(diagonal, line.astype(jnp.float32), 0.0), axis=1, keepdims=True)

    gates = [upright(gate_ref[0, k : k + 1, :]) for k in (0, 1)]
    routes = [upright(route_ref[0, k : k + 1, :]) for k in (0, 1)]
    share = [gate / (gates[0] + gates[1]) for gate in gates]
    for d in (1, 2, 3):
        send(meta.at[d], meta.at[d], m_send.at[d], m_recv.at[d], (g, ahead[d], m)).wait_recv()
    added = jnp.zeros((row_count, quarter), jnp.float32)
    for d in (0, 1, 3, 2):
        expert = ahead[d].astype(jnp.float32)
        scale = jnp.where(routes[0] == expert, share[0], 0.0)
        scale = scale + jnp.where(routes[1] == expert, share[1], 0.0)
        if d == 0:
            came = summed[block(0), :]
        else:
            send(back_got.at[d], back_got.at[d], b_send.at[d], b_recv.at[d],
                 (g, behind[d], m)).wait_recv()
            came = back_got[d]
        added = added + scale * came.astype(jnp.float32)
    own = rows_ref[0, :, cols(m)].astype(jnp.float32) + added
    moe[:, cols(m)] = own.astype(jnp.bfloat16)
    for j in (3, 1, 2):
        go(moe.at[:, cols(m)], moe.at[:, cols(m)], e_send.at[j], e_recv.at[j], (g, e, mp_peer[j]))
    loads[3].wait()

    @pl.when(g == 1)
    def _():
        planes(cache_pairs, cache, 0, cache.shape[0])

    for j in (1, 2, 3):
        theirs = moe.at[:, cols(mp_peer[j])]
        send(theirs, theirs, e_send.at[j], e_recv.at[j], (g, e, mp_peer[j])).wait_recv()
    moe_ref[0] = moe[...]
    encoded = norm_rows(moe[...].astype(jnp.float32), attn_gain_ref[...])

    def kv_copy(d, group, place):
        return send(kv, kv_got.at[kv_block(d), :], k_send.at[d], k_recv.at[d], (group, place, m))

    @pl.when(g == 0)
    def _():
        kv[...] = jnp.dot(encoded, attn[...], preferred_element_type=jnp.float32).astype(
            jnp.bfloat16
        )
        for d in (2, 1, 3, 0):
            kv_copy(d, 1, ahead[d]).start()
        step_ref[0] = encoded
        for d in range(n_expert):
            kv_copy(d, 1, ahead[d]).wait_send()

    @pl.when(g == 1)
    def _():
        query = jnp.dot(
            encoded, attn[:, 0:head_width], preferred_element_type=jnp.float32
        ).astype(jnp.bfloat16)
        positions = cache.shape[0] // row_count
        lane = lax.broadcasted_iota(jnp.int32, (1, total), 1).astype(jnp.float32)
        slot = lax.broadcasted_iota(jnp.int32, (row_count, 1), 0).astype(jnp.float32)
        lengths = upright(cache_len_ref[...])
        row_slot = jnp.full((1, total), -1.0, jnp.float32)
        first_slot = (e * row_count).astype(jnp.float32)
        for d in range(n_expert):
            facts = meta[d].astype(jnp.float32)
            start = jnp.full((1, 1), float(d * row_count), jnp.float32)
            for s in range(src_ref.shape[1]):
                length = facts[0:1, s : s + 1]
                place = facts[1:2, s : s + 1] - first_slot
                here = (lane >= start) & (lane < start + length)
                row_slot = jnp.where(here, place, row_slot)
                lengths = jnp.where(slot == place, 0.0, lengths)
                start = start + length
        shape = (row_count, cache.shape[0])
        offset = lax.broadcasted_iota(
            jnp.int32, shape, 1
        ) - positions * lax.broadcasted_iota(jnp.int32, shape, 0)
        held = (offset >= 0) & (offset < lengths.astype(jnp.int32))
        fresh = slot == row_slot

        def attend(h, pool, inside):
            low, high = h * HEAD_DIM, (h + 1) * HEAD_DIM
            scores = lax.dot_general(
                query[:, low:high], pool[:, low:high], NT, preferred_element_type=jnp.float32
            ) * (1.0 / math.sqrt(HEAD_DIM))
            scores = jnp.where(inside, scores, -1e30)
            highest = jnp.max(scores, axis=-1, keepdims=True)
            raised = jnp.where(inside, jnp.exp(scores - highest), 0.0)
            weight = jnp.sum(raised, axis=-1, keepdims=True)
            probs = (raised / jnp.where(weight > 0.0, weight, 1.0)).astype(jnp.bfloat16)
            return jnp.dot(
                probs, pool[:, head_width + low : head_width + high],
                preferred_element_type=jnp.float32,
            )

        heads = range(head_width // HEAD_DIM)
        from_cache = [attend(h, cache, held) for h in heads]
        for d in range(n_expert):
            kv_copy(d, 1, ahead[d]).wait_recv()
        pieces = [(from_cache[h] + attend(h, kv_got, fresh)).astype(jnp.bfloat16) for h in heads]
        context = jnp.concatenate(pieces, axis=1)

        def mixed_copy(j):
            return send(mixed.at[j], mixed_got.at[j], g_send.at[j], g_recv.at[j],
                        (g, e, mp_peer[j]))

        def final_copy(j, place):
            return send(final.at[:, cols(place)], final.at[:, cols(place)], h_send.at[j],
                        h_recv.at[j], (g, e, mp_peer[j]))

        for j in (3, 1, 2, 0):
            mixed[j] = lax.dot_general(
                context, attn[cols(mp_peer[j]), head_width : 2 * head_width], NT,
                preferred_element_type=jnp.float32,
            ).astype(jnp.bfloat16)
            if j > 0:
                mixed_copy(j).start()
        out = mixed[0].astype(jnp.float32)
        for j in (1, 2, 3):
            mixed_copy(j).wait_recv()
            out = out + mixed_got[j].astype(jnp.float32)
        out = out + moe[:, cols(m)].astype(jnp.float32)
        final[:, cols(m)] = out.astype(jnp.bfloat16)
        for j in (3, 1, 2):
            final_copy(j, m).start()
        for j in (1, 2, 3):
            final_copy(j, mp_peer[j]).wait_recv()
        step_ref[0] = final[...]
        for j in (1, 2, 3):
            mixed_copy(j).wait_send()
            final_copy(j, m).wait_send()

    for copy in pending:
        copy.wait_send()


def dense_body(
    rows, route, gate_int, moe_gain, w_in, w_out, attn_gain, attn_weight, src_len, target, cache,
    cache_len,
):
    row_count, width = rows.shape[1], rows.shape[2]
    n_expert = lax.axis_size("expert")
    total = n_expert * row_count
    units = w_in.shape[3]
    quarter = width // 4
    attn = attn_weight[0]
    kv_cache = cache.reshape(row_count * cache.shape[1], 2, -1)
    both = 2 * attn.shape[2]
    bf16 = jnp.bfloat16
    dma = pltpu.SemaphoreType.DMA
    vmem = pl.BlockSpec(memory_space=pltpu.VMEM)
    hbm = pl.BlockSpec(memory_space=pl.ANY)
    flops = 4 * total * width * units
    return pl.pallas_call(
        kernel,
        out_shape=(jax.ShapeDtypeStruct(rows.shape, bf16), jax.ShapeDtypeStruct(rows.shape, bf16)),
        in_specs=[vmem] * 8 + [hbm] * 4,
        out_specs=(vmem, vmem),
        scratch_shapes=[
            pltpu.VMEM(attn.shape, bf16),
            pltpu.VMEM(kv_cache.shape, bf16),
            pltpu.VMEM((width, both), bf16),
            pltpu.VMEM((kv_cache.shape[0], both), bf16),
            pltpu.VMEM((width, units), bf16),
            pltpu.VMEM((units, width), bf16),
            pltpu.VMEM((total, width), bf16),
            pltpu.VMEM((total, units), bf16),
            pltpu.VMEM((4, total, quarter), bf16),
            pltpu.VMEM((4, total, quarter), bf16),
            pltpu.VMEM((total, quarter), bf16),
            pltpu.VMEM((n_expert, row_count, quarter), bf16),
            pltpu.VMEM((row_count, width), bf16),
            pltpu.VMEM((n_expert, 8, 128), jnp.int32),
            pltpu.VMEM((row_count, both), bf16),
            pltpu.VMEM((total, both), bf16),
            pltpu.VMEM((4, row_count, quarter), bf16),
            pltpu.VMEM((4, row_count, quarter), bf16),
            pltpu.VMEM((row_count, width), bf16),
            dma((4,)),
            dma((n_expert,)), dma((n_expert,)),
            dma((n_expert,)), dma((n_expert,)),
            dma((n_expert, 4)), dma((n_expert, 4)),
            dma((3, 4)), dma((3, 4)),
            dma((n_expert,)), dma((n_expert,)),
            dma((4,)), dma((4,)),
            dma((n_expert,)), dma((n_expert,)),
            dma((4,)), dma((4,)),
            dma((4,)), dma((4,)),
        ],
        compiler_params=pltpu.CompilerParams(
            collective_id=0, has_side_effects=True, vmem_limit_bytes=48 * 1024 * 1024
        ),
        cost_estimate=pl.CostEstimate(flops=flops, bytes_accessed=12 << 20, transcendentals=0),
    )(
        rows, route.transpose(0, 2, 1), gate_int.transpose(0, 2, 1), moe_gain, attn_gain, src_len,
        target, cache_len.reshape(1, -1), w_in, w_out, attn, kv_cache,
    )


def solution(mesh):
    dense = mesh.shape["expert"] == 4 and mesh.shape["mp"] == 4
    return jax.shard_map(
        dense_body if dense else spread_body,
        mesh=mesh,
        in_specs=(
            P("group", "expert", None),
            P("group", "expert", None),
            P("group", "expert", None),
            P("group", None),
            P("group", "expert", None, "mp"),
            P("group", "expert", "mp", None),
            P("group", None),
            P("group", None, None, "mp"),
            P("expert", None),
            P("expert", None),
            P("expert", None, None, "mp"),
            P("expert"),
        ),
        out_specs=(P("group", "expert", None), P("group", "expert", None)),
        check_vma=False,
    )
```

```python
import math

import jax
import jax.numpy as jnp
from jax import lax
from jax.experimental import pallas as pl
from jax.experimental.pallas import tpu as pltpu
from jax.sharding import PartitionSpec as P

HEAD_DIM = 128


def layer_norm(values, gain):
    center = values - jnp.mean(values, axis=-1, keepdims=True)
    spread = jnp.mean(center * center, axis=-1, keepdims=True)
    return center * lax.rsqrt(spread + 1e-05) * gain


def spread_body(
    rows,
    route,
    gate_int,
    moe_gain,
    w_in,
    w_out,
    attn_gain,
    attn_weight,
    src_len,
    target,
    cache,
    cache_len,
):
    experts_count = lax.axis_size("expert")
    row_count = rows.shape[1]
    width = rows.shape[2]
    group_place = lax.axis_index("group")
    expert_place = lax.axis_index("expert")
    capacity = max(2, 4 * row_count // experts_count)
    base = rows[0].astype(jnp.float32)
    normed = layer_norm(base, moe_gain[0]).astype(jnp.bfloat16)
    weights = gate_int[0].astype(jnp.float32)
    weights = weights / jnp.sum(weights, axis=1, keepdims=True)
    flat_dest = route[0].reshape(-1)
    onehot = (flat_dest[:, None] == jnp.arange(experts_count)[None, :]).astype(jnp.int32)
    position = jnp.sum((jnp.cumsum(onehot, axis=0) - 1) * onehot, axis=1)
    flat_index = flat_dest * capacity + position
    pair_index = flat_index.reshape(row_count, 2)
    slot_iota = jnp.arange(experts_count * capacity, dtype=jnp.int32)
    slot_table = (
        (slot_iota[:, None] == pair_index[None, :, 0])
        | (slot_iota[:, None] == pair_index[None, :, 1])
    ).astype(jnp.bfloat16)
    buffer = jnp.dot(slot_table, normed, preferred_element_type=jnp.float32).astype(jnp.bfloat16)
    buffer = buffer.reshape(experts_count, capacity, normed.shape[1])
    hidden = jax.nn.relu(
        jnp.einsum(
            "sci,if->scf",
            lax.all_to_all(buffer, "expert", split_axis=0, concat_axis=0, tiled=True),
            w_in[0, 0],
            preferred_element_type=jnp.float32,
        )
    ).astype(jnp.bfloat16)
    partial_rows = jnp.einsum(
        "scf,fo->sco", hidden, w_out[0, 0], preferred_element_type=jnp.float32
    )
    summed = lax.psum(partial_rows.astype(jnp.bfloat16), "mp")
    returned = lax.all_to_all(summed, "expert", split_axis=0, concat_axis=0, tiled=True)
    returned = returned.reshape(experts_count * capacity, returned.shape[2])
    picked = returned[flat_index].reshape(row_count, 2, returned.shape[1]).astype(jnp.float32)
    added = weights[:, 0:1] * picked[:, 0] + weights[:, 1:2] * picked[:, 1]
    moe_rows = (base + added).astype(jnp.bfloat16)
    encoded = layer_norm(moe_rows.astype(jnp.float32), attn_gain[0]).astype(jnp.bfloat16)
    head_width = attn_weight.shape[3]
    projected = jnp.dot(
        encoded, attn_weight[0].reshape(width, 2 * head_width), preferred_element_type=jnp.float32
    )
    projected = projected.reshape(row_count, 2, head_width).astype(jnp.bfloat16)
    query = projected[:, 0, :]
    lengths = src_len[0]
    ends = jnp.cumsum(lengths)
    starts = ends - lengths
    row_iota = jnp.arange(row_count, dtype=jnp.int32)
    which = jnp.sum((row_iota[:, None] >= ends[None, :]).astype(jnp.int32), axis=1)
    select = which[:, None] == jnp.arange(lengths.shape[0])[None, :]
    row_start = jnp.sum(jnp.where(select, starts[None, :], 0), axis=1)
    row_len = jnp.sum(jnp.where(select, lengths[None, :], 0), axis=1)
    row_slot = jnp.sum(jnp.where(select, target[0][None, :], 0), axis=1)
    row_pos = row_iota - row_start
    positions = cache.shape[1]
    cell_iota = jnp.arange(row_count * positions, dtype=jnp.int32)
    slot_ids = jnp.arange(row_count, dtype=jnp.int32)
    sent_slot = jnp.where(group_place == 0, row_slot, -1)
    slot_kv = cache
    slot_len = cache_len
    kv_piece = lax.all_gather(projected, ("group", "expert"), axis=0, tiled=True)
    slot_piece = lax.all_gather(sent_slot, ("group", "expert"), axis=0, tiled=True)
    pos_piece = lax.all_gather(row_pos, ("group", "expert"), axis=0, tiled=True)
    len_piece = lax.all_gather(row_len, ("group", "expert"), axis=0, tiled=True)
    local = slot_piece - expert_place * row_count
    inside = (local >= 0) & (local < row_count)
    cell = jnp.where(inside, local * positions + pos_piece, -1)
    hit = cell_iota[:, None] == cell[None, :]
    written = jnp.dot(
        hit.astype(jnp.bfloat16),
        kv_piece.reshape(kv_piece.shape[0], -1),
        preferred_element_type=jnp.float32,
    )
    written = written.astype(jnp.bfloat16).reshape(slot_kv.shape)
    touched = jnp.any(hit, axis=1).reshape(row_count, positions)
    slot_kv = jnp.where(touched[:, :, None, None], written, slot_kv)
    slot_hit = (slot_ids[:, None] == local[None, :]) & inside[None, :]
    fresh = jnp.max(jnp.where(slot_hit, len_piece[None, :], 0), axis=1).astype(jnp.int32)
    slot_len = jnp.where(jnp.any(slot_hit, axis=1), fresh, slot_len)
    slot_kv, slot_len = (slot_kv, slot_len)
    heads_here = head_width // HEAD_DIM
    keys = slot_kv[:, :, 0, :].reshape(row_count, positions, heads_here, HEAD_DIM)
    values = slot_kv[:, :, 1, :].reshape(row_count, positions, heads_here, HEAD_DIM)
    heads_query = query.reshape(row_count, heads_here, HEAD_DIM)
    scores = jnp.einsum("thd,tphd->thp", heads_query, keys, preferred_element_type=jnp.float32) * (
        1.0 / math.sqrt(HEAD_DIM)
    )
    inside = jnp.arange(positions)[None, None, :] < slot_len[:, None, None]
    scores = jnp.where(inside, scores, -1e30)
    highest = jnp.max(scores, axis=-1, keepdims=True)
    raised = jnp.where(inside, jnp.exp(scores - highest), 0.0)
    probs = (raised / jnp.sum(raised, axis=-1, keepdims=True)).astype(jnp.bfloat16)
    context = jnp.einsum("thp,tphd->thd", probs, values, preferred_element_type=jnp.float32).astype(
        jnp.bfloat16
    )
    context = context.reshape(row_count, head_width)
    output_map = attn_weight[0][:, 1, :]
    mixed = lax.dot_general(
        context, output_map, (((1,), (1,)), ((), ())), preferred_element_type=jnp.float32
    )
    mixed = lax.psum(mixed.astype(jnp.bfloat16), "mp").astype(jnp.float32)
    decoded = (moe_rows.astype(jnp.float32) + mixed).astype(jnp.bfloat16)
    step_rows = jnp.where(group_place == 0, encoded, decoded)
    return (moe_rows[None], step_rows[None])


MESH = pl.DeviceIdType.MESH
NT = (((1,), (1,)), ((), ()))


def norm_rows(values, gain):
    center = values - jnp.mean(values, axis=-1, keepdims=True)
    spread = jnp.mean(center * center, axis=-1, keepdims=True)
    return (center * lax.rsqrt(spread + 1e-05) * gain).astype(jnp.bfloat16)


def kernel(
    rows_hbm, route_hbm, gate_hbm, moe_gain_hbm, attn_gain_hbm, src_hbm, target_hbm, cache_len_hbm,
    w_in_hbm, w_out_hbm, attn_hbm, cache_hbm,
    moe_ref, step_ref,
    rows_ref, route_ref, gate_ref, moe_gain_ref, attn_gain_ref, src_ref, target_ref, cache_len_ref,
    attn_pairs, cache_pairs, attn, cache, w_in, w_out, gathered, hidden, part, part_got, summed, back_got, moe, meta,
    kv, kv_got, mixed, mixed_got, final,
    load_sem, z_send, z_recv, m_send, m_recv, f_send, f_recv, p_send, p_recv, b_send, b_recv,
    e_send, e_recv, k_send, k_recv, g_send, g_recv, h_send, h_recv,
):
    g = lax.axis_index("group")
    e = lax.axis_index("expert")
    m = lax.axis_index("mp")
    n_expert = lax.axis_size("expert")
    row_count = rows_ref.shape[1]
    width = rows_ref.shape[2]
    quarter = width // 4
    head_width = attn.shape[1] // 2
    total = n_expert * row_count
    y, x = m // 2, m % 2
    mp_peer = (m, y * 2 + 1 - x, (1 - y) * 2 + x, 3 - m)
    ahead = [(e + d) % n_expert for d in range(n_expert)]
    behind = [(e + n_expert - d) % n_expert for d in range(n_expert)]

    loads = [
        pltpu.make_async_copy(w_in_hbm.at[0, 0], w_in, load_sem.at[0]),
        pltpu.make_async_copy(w_out_hbm.at[0, 0], w_out, load_sem.at[1]),
        pltpu.make_async_copy(attn_hbm, attn_pairs, load_sem.at[2]),
        pltpu.make_async_copy(cache_hbm, cache_pairs, load_sem.at[3]),
    ]
    small = (
        (rows_hbm, rows_ref), (moe_gain_hbm, moe_gain_ref), (src_hbm, src_ref),
        (target_hbm, target_ref), (route_hbm, route_ref), (gate_hbm, gate_ref),
        (attn_gain_hbm, attn_gain_ref), (cache_len_hbm, cache_len_ref),
    )
    small_loads = [
        pltpu.make_async_copy(far, near, load_sem.at[4 + i]) for i, (far, near) in enumerate(small)
    ]
    barrier = pltpu.get_barrier_semaphore()
    for load in small_loads:
        load.start()
    friends = [(g, ahead[d], m) for d in range(1, n_expert)]
    friends += [(g, e, mp_peer[j]) for j in (1, 2, 3)]
    friends += [(1 - g, ahead[d], m) for d in range(n_expert)]
    for friend in friends:
        pl.semaphore_signal(barrier, inc=1, device_id=friend, device_id_type=MESH)
    for load in loads:
        load.start()

    def cols(place):
        return pl.ds(pl.multiple_of(place * quarter, quarter), quarter)

    order = (0, 1, 3, 2)
    spans = ((0, 1), (1, 3), (3, 4))

    def block(d):
        return pl.ds(order.index(d) * row_count, row_count)

    def kv_block(d):
        return pl.ds(d * row_count, row_count)

    def span(k):
        low, high = spans[k]
        return pl.ds(low * row_count, (high - low) * row_count)

    def send(src, dst, send_sem, recv_sem, device):
        copy = pltpu.make_async_remote_copy(
            src_ref=src, dst_ref=dst, send_sem=send_sem, recv_sem=recv_sem,
            device_id=device, device_id_type=MESH,
        )
        return copy

    pending = []

    def go(*args):
        copy = send(*args)
        copy.start()
        pending.append(copy)

    for load in small_loads:
        load.wait()
    base = rows_ref[0].astype(jnp.float32)
    gathered[block(0), :] = norm_rows(base, moe_gain_ref[...])
    meta[0] = jnp.zeros(meta.shape[1:], jnp.int32)
    meta[0, 0:1, 0:src_ref.shape[1]] = src_ref[...]
    meta[0, 1:2, 0:src_ref.shape[1]] = target_ref[...]
    pl.semaphore_wait(barrier, len(friends))

    def z_copy(d):
        return send(gathered.at[block(0), cols(m)], gathered.at[block(d), cols(m)],
                    z_send.at[d], z_recv.at[d], (g, ahead[d], m))

    def forward(d):
        mine = gathered.at[block(d), cols(m)]
        z_copy(d).wait_recv()
        for j in (3, 1, 2):
            go(mine, mine, f_send.at[d, j], f_recv.at[d, j], (g, e, mp_peer[j]))

    def forwarded(d):
        for j in (1, 2, 3):
            theirs = gathered.at[block(d), cols(mp_peer[j])]
            send(theirs, theirs, f_send.at[d, j], f_recv.at[d, j], (g, e, mp_peer[j])).wait_recv()

    tile = 256

    def first_product(k):
        def step(n, carry):
            at = pl.ds(pl.multiple_of(n * tile, tile), tile)
            raw = jnp.dot(gathered[span(k), :], w_in[:, at], preferred_element_type=jnp.float32)
            hidden[span(k), at] = jnp.maximum(raw, 0.0).astype(jnp.bfloat16)
            return carry

        lax.fori_loop(0, w_in.shape[1] // tile, step, 0)

    def part_copy(k, j):
        return send(part.at[j, span(k), :], part_got.at[j, span(k), :], p_send.at[k, j],
                    p_recv.at[k, j], (g, e, mp_peer[j]))

    def second_product(k):
        for j in (3, 1, 2, 0):
            part[j, span(k), :] = jnp.dot(
                hidden[span(k), :], w_out[:, cols(mp_peer[j])], preferred_element_type=jnp.float32
            ).astype(jnp.bfloat16)
            if j > 0:
                pending.append(part_copy(k, j))
                pending[-1].start()

    def add_parts(k):
        for j in (1, 2, 3):
            part_copy(k, j).wait_recv()
        for d in order[spans[k][0] : spans[k][1]]:
            at = block(d)
            whole = part[0, at, :].astype(jnp.float32)
            for j in (1, 2, 3):
                whole = whole + part_got[j, at, :].astype(jnp.float32)
            summed[at, :] = whole.astype(jnp.bfloat16)
            if d > 0:
                go(summed.at[at, :], back_got.at[d], b_send.at[d], b_recv.at[d], (g, behind[d], m))

    def planes(pairs, flat, low, high):
        rows_at_once = 64

        def step(i, carry):
            at = pl.ds(pl.multiple_of(i * rows_at_once, rows_at_once), rows_at_once)
            for plane in (0, 1):
                flat[at, plane * head_width : (plane + 1) * head_width] = pairs[at, plane, :]
            return carry

        lax.fori_loop(low // rows_at_once, high // rows_at_once, step, 0)

    for d in (1, 3, 2):
        pending.append(z_copy(d))
        pending[-1].start()
    for d in (1, 2, 3):
        go(meta.at[0], meta.at[d], m_send.at[d], m_recv.at[d], (g, ahead[d], m))
    loads[0].wait()
    first_product(0)
    forward(1)
    forward(3)
    loads[1].wait()
    second_product(0)
    forward(2)
    loads[2].wait()
    planes(attn_pairs, attn, 0, width // 2)
    forwarded(1)
    forwarded(3)
    first_product(1)
    add_parts(0)
    second_product(1)
    forwarded(2)
    first_product(2)
    second_product(2)
    add_parts(1)
    planes(attn_pairs, attn, width // 2, 3 * width // 4)
    add_parts(2)
    planes(attn_pairs, attn, 3 * width // 4, width)

    square = (row_count, row_count)
    diagonal = lax.broadcasted_iota(jnp.int32, square, 0) == lax.broadcasted_iota(
        jnp.int32, square, 1
    )

    def upright(line):
        return jnp.sum(jnp.where(diagonal, line.astype(jnp.float32), 0.0), axis=1, keepdims=True)

    gates = [upright(gate_ref[0, k : k + 1, :]) for k in (0, 1)]
    routes = [upright(route_ref[0, k : k + 1, :]) for k in (0, 1)]
    share = [gate / (gates[0] + gates[1]) for gate in gates]
    for d in (1, 2, 3):
        send(meta.at[d], meta.at[d], m_send.at[d], m_recv.at[d], (g, ahead[d], m)).wait_recv()
    added = jnp.zeros((row_count, quarter), jnp.float32)
    for d in (0, 1, 3, 2):
        expert = ahead[d].astype(jnp.float32)
        scale = jnp.where(routes[0] == expert, share[0], 0.0)
        scale = scale + jnp.where(routes[1] == expert, share[1], 0.0)
        if d == 0:
            came = summed[block(0), :]
        else:
            send(back_got.at[d], back_got.at[d], b_send.at[d], b_recv.at[d],
                 (g, behind[d], m)).wait_recv()
            came = back_got[d]
        added = added + scale * came.astype(jnp.float32)
    own = rows_ref[0, :, cols(m)].astype(jnp.float32) + added
    moe[:, cols(m)] = own.astype(jnp.bfloat16)
    for j in (3, 1, 2):
        go(moe.at[:, cols(m)], moe.at[:, cols(m)], e_send.at[j], e_recv.at[j], (g, e, mp_peer[j]))
    loads[3].wait()

    @pl.when(g == 1)
    def _():
        planes(cache_pairs, cache, 0, cache.shape[0])

    for j in (1, 2, 3):
        theirs = moe.at[:, cols(mp_peer[j])]
        send(theirs, theirs, e_send.at[j], e_recv.at[j], (g, e, mp_peer[j])).wait_recv()
    moe_ref[0] = moe[...]
    encoded = norm_rows(moe[...].astype(jnp.float32), attn_gain_ref[...])

    def kv_copy(d, group, place):
        return send(kv, kv_got.at[kv_block(d), :], k_send.at[d], k_recv.at[d], (group, place, m))

    @pl.when(g == 0)
    def _():
        kv[...] = jnp.dot(encoded, attn[...], preferred_element_type=jnp.float32).astype(
            jnp.bfloat16
        )
        for d in (2, 1, 3, 0):
            kv_copy(d, 1, ahead[d]).start()
        step_ref[0] = encoded
        for d in range(n_expert):
            kv_copy(d, 1, ahead[d]).wait_send()

    @pl.when(g == 1)
    def _():
        query = jnp.dot(
            encoded, attn[:, 0:head_width], preferred_element_type=jnp.float32
        ).astype(jnp.bfloat16)
        positions = cache.shape[0] // row_count
        lane = lax.broadcasted_iota(jnp.int32, (1, total), 1).astype(jnp.float32)
        slot = lax.broadcasted_iota(jnp.int32, (row_count, 1), 0).astype(jnp.float32)
        lengths = upright(cache_len_ref[...])
        row_slot = jnp.full((1, total), -1.0, jnp.float32)
        first_slot = (e * row_count).astype(jnp.float32)
        for d in range(n_expert):
            facts = meta[d].astype(jnp.float32)
            start = jnp.full((1, 1), float(d * row_count), jnp.float32)
            for s in range(src_ref.shape[1]):
                length = facts[0:1, s : s + 1]
                place = facts[1:2, s : s + 1] - first_slot
                here = (lane >= start) & (lane < start + length)
                row_slot = jnp.where(here, place, row_slot)
                lengths = jnp.where(slot == place, 0.0, lengths)
                start = start + length
        shape = (row_count, cache.shape[0])
        offset = lax.broadcasted_iota(
            jnp.int32, shape, 1
        ) - positions * lax.broadcasted_iota(jnp.int32, shape, 0)
        held = (offset >= 0) & (offset < lengths.astype(jnp.int32))
        fresh = slot == row_slot

        def attend(h, pool, inside):
            low, high = h * HEAD_DIM, (h + 1) * HEAD_DIM
            scores = lax.dot_general(
                query[:, low:high], pool[:, low:high], NT, preferred_element_type=jnp.float32
            ) * (1.0 / math.sqrt(HEAD_DIM))
            scores = jnp.where(inside, scores, -1e30)
            highest = jnp.max(scores, axis=-1, keepdims=True)
            raised = jnp.where(inside, jnp.exp(scores - highest), 0.0)
            weight = jnp.sum(raised, axis=-1, keepdims=True)
            probs = (raised / jnp.where(weight > 0.0, weight, 1.0)).astype(jnp.bfloat16)
            return jnp.dot(
                probs, pool[:, head_width + low : head_width + high],
                preferred_element_type=jnp.float32,
            )

        heads = range(head_width // HEAD_DIM)
        from_cache = [attend(h, cache, held) for h in heads]
        for d in range(n_expert):
            kv_copy(d, 1, ahead[d]).wait_recv()
        pieces = [(from_cache[h] + attend(h, kv_got, fresh)).astype(jnp.bfloat16) for h in heads]
        context = jnp.concatenate(pieces, axis=1)

        def mixed_copy(j):
            return send(mixed.at[j], mixed_got.at[j], g_send.at[j], g_recv.at[j],
                        (g, e, mp_peer[j]))

        def final_copy(j, place):
            return send(final.at[:, cols(place)], final.at[:, cols(place)], h_send.at[j],
                        h_recv.at[j], (g, e, mp_peer[j]))

        for j in (3, 1, 2, 0):
            mixed[j] = lax.dot_general(
                context, attn[cols(mp_peer[j]), head_width : 2 * head_width], NT,
                preferred_element_type=jnp.float32,
            ).astype(jnp.bfloat16)
            if j > 0:
                mixed_copy(j).start()
        out = mixed[0].astype(jnp.float32)
        for j in (1, 2, 3):
            mixed_copy(j).wait_recv()
            out = out + mixed_got[j].astype(jnp.float32)
        out = out + moe[:, cols(m)].astype(jnp.float32)
        final[:, cols(m)] = out.astype(jnp.bfloat16)
        for j in (3, 1, 2):
            final_copy(j, m).start()
        for j in (1, 2, 3):
            final_copy(j, mp_peer[j]).wait_recv()
        step_ref[0] = final[...]
        for j in (1, 2, 3):
            mixed_copy(j).wait_send()
            final_copy(j, m).wait_send()

    for copy in pending:
        copy.wait_send()


def dense_body(
    rows, route, gate_int, moe_gain, w_in, w_out, attn_gain, attn_weight, src_len, target, cache,
    cache_len,
):
    row_count, width = rows.shape[1], rows.shape[2]
    n_expert = lax.axis_size("expert")
    total = n_expert * row_count
    units = w_in.shape[3]
    quarter = width // 4
    attn = attn_weight[0]
    kv_cache = cache.reshape(row_count * cache.shape[1], 2, -1)
    both = 2 * attn.shape[2]
    bf16 = jnp.bfloat16
    dma = pltpu.SemaphoreType.DMA
    vmem = pl.BlockSpec(memory_space=pltpu.VMEM)
    hbm = pl.BlockSpec(memory_space=pltpu.HBM)
    near = [
        rows, route.transpose(0, 2, 1), gate_int.transpose(0, 2, 1), moe_gain, attn_gain, src_len,
        target, cache_len.reshape(1, -1),
    ]
    flops = 4 * total * width * units
    return pl.pallas_call(
        kernel,
        out_shape=(jax.ShapeDtypeStruct(rows.shape, bf16), jax.ShapeDtypeStruct(rows.shape, bf16)),
        in_specs=[hbm] * 12,
        out_specs=(vmem, vmem),
        scratch_shapes=[
            *[pltpu.VMEM(array.shape, array.dtype) for array in near],
            pltpu.VMEM(attn.shape, bf16),
            pltpu.VMEM(kv_cache.shape, bf16),
            pltpu.VMEM((width, both), bf16),
            pltpu.VMEM((kv_cache.shape[0], both), bf16),
            pltpu.VMEM((width, units), bf16),
            pltpu.VMEM((units, width), bf16),
            pltpu.VMEM((total, width), bf16),
            pltpu.VMEM((total, units), bf16),
            pltpu.VMEM((4, total, quarter), bf16),
            pltpu.VMEM((4, total, quarter), bf16),
            pltpu.VMEM((total, quarter), bf16),
            pltpu.VMEM((n_expert, row_count, quarter), bf16),
            pltpu.VMEM((row_count, width), bf16),
            pltpu.VMEM((n_expert, 8, 128), jnp.int32),
            pltpu.VMEM((row_count, both), bf16),
            pltpu.VMEM((total, both), bf16),
            pltpu.VMEM((4, row_count, quarter), bf16),
            pltpu.VMEM((4, row_count, quarter), bf16),
            pltpu.VMEM((row_count, width), bf16),
            dma((12,)),
            dma((n_expert,)), dma((n_expert,)),
            dma((n_expert,)), dma((n_expert,)),
            dma((n_expert, 4)), dma((n_expert, 4)),
            dma((3, 4)), dma((3, 4)),
            dma((n_expert,)), dma((n_expert,)),
            dma((4,)), dma((4,)),
            dma((n_expert,)), dma((n_expert,)),
            dma((4,)), dma((4,)),
            dma((4,)), dma((4,)),
        ],
        compiler_params=pltpu.CompilerParams(
            collective_id=0, has_side_effects=True, vmem_limit_bytes=63 * 1024 * 1024
        ),
        cost_estimate=pl.CostEstimate(flops=flops, bytes_accessed=12 << 20, transcendentals=0),
    )(
        *near, w_in, w_out, attn, kv_cache,
    )


def solution(mesh):
    dense = mesh.shape["expert"] == 4 and mesh.shape["mp"] == 4
    return jax.shard_map(
        dense_body if dense else spread_body,
        mesh=mesh,
        in_specs=(
            P("group", "expert", None),
            P("group", "expert", None),
            P("group", "expert", None),
            P("group", None),
            P("group", "expert", None, "mp"),
            P("group", "expert", "mp", None),
            P("group", None),
            P("group", None, None, "mp"),
            P("expert", None),
            P("expert", None),
            P("expert", None, None, "mp"),
            P("expert"),
        ),
        out_specs=(P("group", "expert", None), P("group", "expert", None)),
        check_vma=False,
    )
```
